32 devices in a mesh: region: 4 (over z), dev: 8 (over y, x, core).
Axes of the slice: x: 2, y: 2, z: 4, core: 2. Of those that a mesh axis runs over, the one named last changes fastest.
Arguments:
- loads: float32 [256, 32, 1024], P(('region', 'dev')), may hold values from -50 to 50
- factor: bfloat16 [256, 1024, 1024], P(('region', 'dev')), may hold values from -1 to 1, as said below
- pivots: float32 [256, 1024], P(('region', 'dev')), may hold values from 0.04 to 0.14, as said below
- lower: float32 [256, 1024], P(('region', 'dev')), may hold values from -1 to -0.2
- upper: float32 [256, 1024], P(('region', 'dev')), may hold values from 0.2 to 1
- incidence: int32 [256, 16], P(('region', 'dev')), may hold values from 0 to 511, as said below
- counts: int32 [256], P(('region', 'dev')), may hold values from 8 to 16, as said below
Outputs:
- dispatch: float32 [256, 32, 1024], P(('region', 'dev'))
- duals: float32 [256, 16, 128], P(('region', 'dev'))
- residuals: float32 [14, 2], replicated
The draws below stay inside these ranges and needn't reach their ends.
Inputs may be any that keep to these rules, and one draw needn't show every extreme that they name: `incidence`: slot j of area a is live when j < counts[a]. Bus b is owned by device b // 16, devices numbered region-major. The live slots of one device name at most 16 buses owned by any one device of its own region and at most 8 buses owned in any one other region; in every draw every device reaches both bounds. A bus owned in another region is owned by the device with the same dev index there. `counts`: among the 8 areas of each device one has 16 live slots and the others at least 8. `factor`: unit lower triangular: ones on the diagonal, zeros above it. Rows below 64 of every area have inverse pivots of 0.10 or more; the other rows have them up to 0.14 as well.
All inputs are finite; a program needn't handle non-finite values.
Results may differ from the reference program's by a relative error of at most 0.005.
Values sent between devices are 32-bit elements; how exact they have to be, the bound alone decides.
A program may use at most 64 MiB of HBM per device.

```python
import math
import jax
import jax.numpy as jnp
from jax import lax

K = 1024
S = 32
ROWS_SLOT = 4
BVAL = 128
NB = 16
AREA_DEV = 8
BUS_DEV = 16
CAP_IN = 16
CAP_X = 8
ITERS = 14
AREAS = 256
NBUS = 512
N_REGION = 4
N_DEV = 8


def device_buses(dev_key, device_index, area_counts):
    key_order, key_first, key_shift, key_pool, key_pick = jax.random.split(dev_key, 5)
    item_count = AREA_DEV * NB
    region_now = device_index // N_DEV
    column_now = device_index % N_DEV
    live_slot = (jnp.arange(NB)[None, :] < area_counts[:, None]).reshape(item_count)
    scores = jnp.where(live_slot, 0, item_count) + jax.random.permutation(key_order, item_count)
    ordering = jnp.argsort(scores)
    rank_of = jnp.argsort(ordering)
    first_peer = jax.random.randint(key_first, (), 0, N_DEV)
    far_shift = jax.random.randint(key_shift, (), 0, N_REGION - 1)
    far_region = (region_now + 1 + far_shift) % N_REGION
    peer_list = (first_peer + 1 + jnp.arange(N_DEV - 1)) % N_DEV
    near_pool = jnp.repeat(region_now * N_DEV + peer_list, CAP_IN)
    offsets = 1 + (far_shift + 1 + jnp.arange(N_REGION - 2)) % (N_REGION - 1)
    far_pool = jnp.repeat((region_now + offsets) % N_REGION * N_DEV + column_now, CAP_X)
    spare_pool = jax.random.permutation(key_pool, jnp.concatenate([near_pool, far_pool]))
    sequence = jnp.concatenate([jnp.full((CAP_IN,), region_now * N_DEV + first_peer), jnp.full((CAP_X,), far_region * N_DEV + column_now), spare_pool, jnp.full((item_count,), region_now * N_DEV + first_peer)])[:item_count]
    owner_dev = sequence[rank_of]
    bus_local = jax.random.randint(key_pick, (item_count,), 0, BUS_DEV)
    return (owner_dev * BUS_DEV + bus_local).astype(jnp.int32)


def routing_plan(key):
    devices = N_REGION * N_DEV
    key_count, key_full, key_devs = jax.random.split(key, 3)
    area_counts = jax.random.randint(key_count, (devices, AREA_DEV), NB // 2, NB + 1)
    full_area = jax.random.randint(key_full, (devices,), 0, AREA_DEV)
    area_counts = jnp.where(jnp.arange(AREA_DEV)[None, :] == full_area[:, None], NB, area_counts).astype(jnp.int32)
    device_keys = jax.random.split(key_devs, devices)
    bus_ids = jax.vmap(device_buses)(device_keys, jnp.arange(devices, dtype=jnp.int32), area_counts)
    return (area_counts.reshape(AREAS), bus_ids.reshape(AREAS, NB))


def draw_counts(key, part):
    return routing_plan(key)[0]


def draw_incidence(key, part):
    return routing_plan(key)[1]


def draw_factor(key, part):
    key = jax.random.fold_in(key, 11)
    spread = 0.6 / math.sqrt(K)
    below = jnp.arange(K)[:, None] > jnp.arange(K)[None, :]
    noise = jax.random.uniform(key, (AREAS, K, K), jnp.float32, -spread, spread)
    result = jnp.where(below[None, :, :], noise, 0.0) + jnp.eye(K, dtype=jnp.float32)[None, :, :]
    return result.astype(jnp.bfloat16)


def draw_pivots(key, part):
    key = jax.random.fold_in(key, 7)
    key_edge, key_rest = jax.random.split(key)
    edge_rows = jnp.arange(K)[None, :] < NB * ROWS_SLOT
    edge_value = jnp.exp(jax.random.uniform(key_edge, (AREAS, K), jnp.float32, math.log(0.1), math.log(0.14)))
    rest_value = jnp.exp(jax.random.uniform(key_rest, (AREAS, K), jnp.float32, math.log(0.04), math.log(0.14)))
    return jnp.clip(jnp.where(edge_rows, edge_value, rest_value), 0.04, 0.14)


def draw_loads(key, part):
    key = jax.random.fold_in(key, 5)
    key_rough, key_base = jax.random.split(key)
    rising = 1.0 + 2.0 * jnp.arange(AREAS, dtype=jnp.float32) / max(AREAS - 1, 1)
    rough = jnp.exp(jax.random.uniform(key_rough, (AREAS, 1, K), jnp.float32, 0.0, math.log(4.0)))
    base = jnp.clip(jax.random.normal(key_base, (AREAS, S, K), jnp.float32), -4.0, 4.0)
    return 0.6 * rising[:, None, None] * rough * base


def block_levels(key, dims, cuts, low, top_value):
    gain = 1.0
    for axis_at, shards_of in cuts:
        heights = jax.random.uniform(jax.random.fold_in(jax.random.fold_in(key, 6), axis_at), (shards_of,), jnp.float32, low / len(cuts), top_value / len(cuts))
        gain = gain * jnp.repeat(jnp.exp(heights), dims[axis_at] // shards_of).reshape((-1,) + (1,) * (len(dims) - 1 - axis_at))
    return gain


def setup_inputs(seed: int = 0) -> dict:
    splits = jax.random.split(jax.random.key(seed), 8)
    loads = draw_loads(jax.random.fold_in(splits[7], 71), 0)
    factor = draw_factor(jax.random.fold_in(splits[7], 71), 0)
    pivots = draw_pivots(jax.random.fold_in(splits[7], 71), 0)
    lower = jnp.clip(-1.0 + 0.8 * jax.random.uniform(splits[3], (AREAS, K), jnp.float32) ** block_levels(splits[3], (AREAS, K), ((0, 32),), -0.2, 0.2), -1.0, -0.2)
    upper = jnp.clip(0.2 + 0.8 * jax.random.uniform(splits[4], (AREAS, K), jnp.float32) ** block_levels(splits[4], (AREAS, K), ((0, 32),), -0.2, 0.2), 0.2, 1.0)
    incidence = draw_incidence(jax.random.fold_in(splits[7], 71), 0)
    counts = draw_counts(jax.random.fold_in(splits[7], 71), 0)
    return dict(loads=loads, factor=factor, pivots=pivots, lower=lower, upper=upper, incidence=incidence, counts=counts)


RHO = 4.0
SIGMA = 1.0


def to_blocks(state_field):
    leading = state_field[:, :, :NB * ROWS_SLOT].reshape(state_field.shape[0], S, NB, ROWS_SLOT)
    return jnp.transpose(leading, (0, 2, 1, 3)).reshape(state_field.shape[0], NB, BVAL)


def from_blocks(blocks):
    leading = jnp.transpose(blocks.reshape(blocks.shape[0], NB, S, ROWS_SLOT), (0, 2, 1, 3))
    leading = leading.reshape(blocks.shape[0], S, NB * ROWS_SLOT)
    return jnp.pad(leading, ((0, 0), (0, 0), (0, K - NB * ROWS_SLOT)))


def solve_area(packed):
    right_side, factor_one, pivot_one = packed
    forward = jnp.dot(right_side.astype(jnp.bfloat16), factor_one.T, preferred_element_type=jnp.float32)
    scaled = (forward * pivot_one[None, :]).astype(jnp.bfloat16)
    return jnp.dot(scaled, factor_one, preferred_element_type=jnp.float32)


def reference(loads, factor, pivots, lower, upper, incidence, counts):
    live_slot = (jnp.arange(NB)[None, :] < counts[:, None]).astype(jnp.float32)[:, :, None]
    flat_bus = incidence.reshape(-1)
    bus_count = jax.ops.segment_sum(live_slot.reshape(-1), flat_bus, num_segments=NBUS)
    bus_count = jnp.maximum(bus_count, 1.0)
    duals = jnp.zeros((AREAS, NB, BVAL), jnp.float32)
    z_slot = jnp.zeros((AREAS, NB, BVAL), jnp.float32)
    clipped = jnp.zeros_like(loads)
    offset = jnp.zeros_like(loads)
    z_prev = jnp.zeros((NBUS, BVAL), jnp.float32)
    dispatch = jnp.zeros_like(loads)
    history = []
    for step_num in range(ITERS):
        right_side = loads + RHO * from_blocks(live_slot * (z_slot - duals)) + SIGMA * (clipped - offset)
        dispatch = lax.map(solve_area, (right_side, factor, pivots))
        clipped_new = jnp.clip(dispatch + offset, lower[:, None, :], upper[:, None, :])
        offset = offset + dispatch - clipped_new
        clipped = clipped_new
        blocks = to_blocks(dispatch)
        values = live_slot * (blocks + duals)
        z_bus = jax.ops.segment_sum(values.reshape(-1, BVAL), flat_bus, num_segments=NBUS) / bus_count[:, None]
        z_slot = live_slot * z_bus[incidence]
        misfit = live_slot * (blocks - z_slot)
        duals = duals + misfit
        change = z_bus - z_prev
        history.append(jnp.stack([jnp.sum(misfit * misfit), RHO * RHO * jnp.sum(change * change)]))
        z_prev = z_bus
    residuals = jnp.stack(history) / (AREAS * BVAL)
    return dispatch, duals, residuals
```

```python
import functools

import jax
import jax.numpy as jnp
from jax import lax
from jax.experimental import pallas as pl
from jax.experimental.pallas import tpu as pltpu
from jax.sharding import PartitionSpec as P

ROWS_SLOT = 4
BLK = 128
BUS_DEV = 16
ITERS = 14
RHO = 4.0
SIGMA = 1.0
TILE = 256
F32 = jnp.float32
BF16 = jnp.bfloat16
MESH = pl.DeviceIdType.MESH
NT = (((1,), (1,)), ((), ()))
NN = (((1,), (0,)), ((), ()))


def mm(left, right, dims=NN):
    return lax.dot_general(left, right, dims, preferred_element_type=F32)


def split3(x):
    high = x.astype(BF16)
    rest = x - high.astype(F32)
    mid = rest.astype(BF16)
    low = (rest - mid.astype(F32)).astype(BF16)
    return high, mid, low


def kernel(
    n_region, n_dev, area_count, scenarios, order, slots,
    loads_ref, factor_ref, pivots_ref, lower_ref, upper_ref, row_ref, col_ref,
    dispatch_ref, duals_ref, res_ref,
    fac, wide, known, scaled, offset, pick, place, live, rhs_b, base_b, off_b, loads_b, low_b, up_b, blk, duals,
    part, got, table, mean, counts_got, members, res_sum, res_near, res_far,
    fac_sem, send_sem, back_send, got_sem, table_sem, counts_sem, near_sem, far_sem,
):
    me_r = lax.axis_index("region")
    me_d = lax.axis_index("dev")
    items = area_count * slots
    rows = area_count * scenarios
    places = ROWS_SLOT * items
    edge = slots * ROWS_SLOT
    groups = n_dev + n_region
    near = [lax.rem(me_d + step, n_dev) for step in range(1, n_dev)]
    far = [lax.rem(me_r + step, n_region) for step in range(1, n_region)]
    peers = [((me_r, d), d, me_d, d) for d in near]
    peers += [((r, me_d), n_dev + r, n_dev + me_r, n_dev + r) for r in far]

    def factor_copy(area):
        return pltpu.make_async_copy(factor_ref.at[area], fac.at[area], fac_sem.at[area])

    for area in range(area_count):
        factor_copy(area).start()

    got[...] = jnp.zeros_like(got)
    counts_got[...] = jnp.zeros_like(counts_got)
    table[...] = jnp.zeros_like(table)
    res_sum[...] = jnp.zeros_like(res_sum)

    barrier = pltpu.get_barrier_semaphore()
    for device, _, _, _ in peers:
        pl.semaphore_signal(barrier, inc=1, device_id=device, device_id_type=MESH)
    pl.semaphore_wait(barrier, len(peers))

    def group_rows(index):
        return pl.ds(pl.multiple_of(index * BUS_DEV, BUS_DEV), BUS_DEV)

    def outgoing(number, target, semaphores):
        device, theirs, mine, _ = peers[number]
        return pltpu.make_async_remote_copy(
            src_ref=part.at[group_rows(theirs)], dst_ref=target.at[group_rows(mine)],
            send_sem=send_sem.at[number], recv_sem=semaphores.at[mine],
            device_id=device, device_id_type=MESH,
        )

    def incoming(number, target, semaphores):
        device, theirs, _, here = peers[number]
        return pltpu.make_async_remote_copy(
            src_ref=part.at[group_rows(theirs)], dst_ref=target.at[group_rows(here)],
            send_sem=send_sem.at[number], recv_sem=semaphores.at[here],
            device_id=device, device_id_type=MESH,
        )

    def back(number, here=False):
        device, _, mine, theirs = peers[number]
        at = theirs if here else mine
        return pltpu.make_async_remote_copy(
            src_ref=mean, dst_ref=table.at[group_rows(at)],
            send_sem=back_send.at[number], recv_sem=table_sem.at[at],
            device_id=device, device_id_type=MESH,
        )

    def group_sum(ref):
        total = ref[0:BUS_DEV, :]
        for index in range(1, groups):
            total = total + ref[index * BUS_DEV : (index + 1) * BUS_DEV, :]
        return total

    picked = lax.broadcasted_iota(jnp.int32, (groups * BUS_DEV, items), 0) == row_ref[...]
    picked = jnp.where(picked, 1.0, 0.0)
    part[...] = jnp.broadcast_to(jnp.sum(picked, axis=1, keepdims=True), part.shape)
    for number in range(len(peers)):
        outgoing(number, counts_got, counts_sem).start()
    pick[...] = picked.astype(BF16)
    placed = lax.broadcasted_iota(jnp.int32, (items, groups * BUS_DEV), 1) == col_ref[...]
    place[...] = jnp.where(placed, 1.0, 0.0).astype(BF16)
    live[...] = jnp.broadcast_to(jnp.where(col_ref[...] >= 0, 1.0, 0.0), live.shape)
    counts_got[group_rows(me_d), :] = part[group_rows(me_d), :]

    source = lax.broadcasted_iota(jnp.int32, (area_count * BLK, places), 0)
    target = lax.broadcasted_iota(jnp.int32, (area_count * BLK, places), 1)
    slot_of = lax.rem(target, slots)
    area_of = lax.rem(target // slots, area_count)
    row_of = target // items
    order_hot = jnp.where(source == area_of * BLK + slot_of * ROWS_SLOT + row_of, 1.0, 0.0).astype(BF16)

    def stack_rows(x):
        return jnp.concatenate([x[:, r * items : (r + 1) * items] for r in range(ROWS_SLOT)], axis=0)

    def to_blocks(x):
        parts = [mm(piece, order_hot) for piece in split3(x)]
        return stack_rows(parts[0] + parts[1] + parts[2]).T

    loads_b[...] = to_blocks(jnp.concatenate([loads_ref[a, :, :BLK] for a in range(area_count)], axis=1))
    for bound, kept in ((lower_ref, low_b), (upper_ref, up_b)):
        line = jnp.concatenate([bound[a : a + 1, :BLK] for a in range(area_count)], axis=1)
        kept[...] = to_blocks(jnp.broadcast_to(line, (scenarios, area_count * BLK)))

    column = lax.broadcasted_iota(jnp.int32, (scenarios, TILE), 1)
    tiles = order // TILE

    def forward_known(area, pieces):
        for c in range(tiles):
            here = jnp.concatenate(pieces[: c + 1], axis=1) if c else pieces[0]
            known[pl.ds(area * scenarios, scenarios), c * TILE : (c + 1) * TILE] = mm(
                here, fac[area, c * TILE : (c + 1) * TILE, : (c + 1) * TILE], NT
            )

    def first(area, carry):
        factor_copy(area).wait()
        pieces = []
        for c in range(tiles):
            value = loads_ref[area, :, c * TILE : (c + 1) * TILE]
            if c == 0:
                value = jnp.where(column < edge, 0.0, value)
            pieces.append(value.astype(BF16))
        forward_known(area, pieces)
        return carry

    lax.fori_loop(0, area_count, first, 0)

    def gather_wide(chunk, carry):
        at = pl.ds(pl.multiple_of(chunk * TILE, TILE), TILE)
        joined = jnp.concatenate([fac[a, at, :BLK] for a in range(area_count)], axis=1)
        wide[at, :] = mm(joined, order_hot).astype(BF16)
        return carry

    lax.fori_loop(0, tiles, gather_wide, 0)

    offset[...] = jnp.zeros_like(offset)
    off_b[...] = jnp.zeros_like(off_b)
    duals[...] = jnp.zeros_like(duals)
    mean[...] = jnp.zeros_like(mean)
    rhs_b[...] = loads_b[...]

    for number in range(len(peers)):
        incoming(number, counts_got, counts_sem).wait_recv()
        outgoing(number, counts_got, counts_sem).wait_send()
    members[...] = jnp.maximum(group_sum(counts_got), 1.0)

    own_area = lax.broadcasted_iota(jnp.int32, (scenarios, places), 1)
    own_area = lax.rem(own_area // slots, area_count)

    def interior(area, carry):
        at = pl.ds(pl.multiple_of(area * scenarios, scenarios), scenarios)
        pieces = []
        for c in range(tiles):
            cols = slice(c * TILE, (c + 1) * TILE)
            found = mm(scaled[at, c * TILE :], fac[area, c * TILE :, cols])
            dispatch_ref[area, :, cols] = found
            moved = found + offset[at, cols]
            boxed = jnp.clip(moved, lower_ref[pl.ds(area, 1), cols], upper_ref[pl.ds(area, 1), cols])
            rest = moved - boxed
            offset[at, cols] = rest
            value = loads_ref[area, :, cols] + SIGMA * (boxed - rest)
            if c == 0:
                value = jnp.where(column < edge, 0.0, value)
            pieces.append(value.astype(BF16))
        forward_known(area, pieces)
        return carry

    def iterate(step, carry):
        turned = rhs_b[...].T
        flat = jnp.concatenate(
            [turned[r * scenarios : (r + 1) * scenarios, :] for r in range(ROWS_SLOT)], axis=1
        )
        left = jnp.concatenate(
            [jnp.where(own_area == a, flat, 0.0) for a in range(area_count)], axis=0
        ).astype(BF16)
        for c in range(tiles):
            cols = slice(c * TILE, (c + 1) * TILE)
            forward = known[:, cols] + mm(left, wide[cols, :], NT)
            forward = forward.reshape(area_count, scenarios, TILE) * pivots_ref[:, cols][:, None, :]
            scaled[:, cols] = forward.reshape(rows, TILE).astype(BF16)
        product = mm(scaled[...], wide[...])
        total = jnp.zeros((scenarios, places), F32)
        for a in range(area_count):
            total = total + jnp.where(own_area == a, product[a * scenarios : (a + 1) * scenarios, :], 0.0)
        block = stack_rows(total).T
        blk[...] = block
        values = (block + duals[...]) * live[...]
        pieces = split3(values)
        part[...] = mm(pick[...], pieces[0]) + mm(pick[...], pieces[1]) + mm(pick[...], pieces[2])
        for number in range(len(peers)):
            outgoing(number, got, got_sem).start()
        got[group_rows(me_d), :] = part[group_rows(me_d), :]
        moved = block + off_b[...]
        boxed = jnp.clip(moved, low_b[...], up_b[...])
        rest = moved - boxed
        off_b[...] = rest
        base_b[...] = loads_b[...] + SIGMA * (boxed - rest)

        lax.fori_loop(0, area_count // 2, interior, 0)

        for number in range(len(peers)):
            incoming(number, got, got_sem).wait_recv()
        fresh = group_sum(got) / members[...]
        change = fresh - mean[...]
        mean[...] = fresh
        for number in range(len(peers)):
            back(number).start()
        table[group_rows(me_d), :] = fresh
        res_sum[pl.ds(16 + step, 1), :] = (RHO * RHO) * jnp.sum(change * change, axis=0, keepdims=True)

        lax.fori_loop(area_count // 2, area_count, interior, 0)

        for number in range(len(peers)):
            back(number, here=True).wait_recv()
        pieces = split3(table[...])
        z_slot = mm(place[...], pieces[0]) + mm(place[...], pieces[1]) + mm(place[...], pieces[2])
        gap = (blk[...] - z_slot) * live[...]
        fresh_duals = duals[...] + gap
        duals[...] = fresh_duals
        rhs_b[...] = base_b[...] + RHO * (live[...] * (z_slot - fresh_duals))
        res_sum[pl.ds(step, 1), :] = jnp.sum(gap * gap, axis=0, keepdims=True)
        for number in range(len(peers)):
            outgoing(number, got, got_sem).wait_send()
            back(number).wait_send()
        return carry

    lax.fori_loop(0, ITERS, iterate, 0)

    def near_copy(number, here=False):
        device, _, mine, theirs = peers[number]
        at = theirs if here else mine
        return pltpu.make_async_remote_copy(
            src_ref=res_sum, dst_ref=res_near.at[at],
            send_sem=send_sem.at[number], recv_sem=near_sem.at[at], device_id=device, device_id_type=MESH,
        )

    def far_copy(number, here=False):
        device, _, mine, theirs = peers[number]
        at = (theirs if here else mine) - n_dev
        return pltpu.make_async_remote_copy(
            src_ref=res_sum, dst_ref=res_far.at[at],
            send_sem=send_sem.at[number], recv_sem=far_sem.at[at], device_id=device, device_id_type=MESH,
        )

    nears = range(n_dev - 1)
    fars = range(n_dev - 1, len(peers))
    for number in nears:
        near_copy(number).start()
    res_near[pl.ds(me_d, 1)] = res_sum[...][None]
    lane_from = lax.broadcasted_iota(jnp.int32, (BLK, BLK), 0)
    lane_to = lax.broadcasted_iota(jnp.int32, (BLK, BLK), 1)
    wanted = lax.rem(lane_to, ROWS_SLOT) * scenarios + lane_to // ROWS_SLOT
    lanes_hot = jnp.where(lane_from == wanted, 1.0, 0.0).astype(BF16)
    pieces = split3(duals[...])
    duals_ref[...] = mm(pieces[0], lanes_hot) + mm(pieces[1], lanes_hot) + mm(pieces[2], lanes_hot)
    for number in nears:
        near_copy(number, here=True).wait_recv()
        near_copy(number).wait_send()
    total = res_near[0]
    for index in range(1, n_dev):
        total = total + res_near[index]
    res_sum[...] = total
    for number in fars:
        far_copy(number).start()
    res_far[pl.ds(me_r, 1)] = total[None]
    for number in fars:
        far_copy(number, here=True).wait_recv()
        far_copy(number).wait_send()
    total = res_far[0]
    for index in range(1, n_region):
        total = total + res_far[index]
    sums = jnp.sum(total, axis=1, keepdims=True) / float(area_count * n_dev * n_region * BLK)
    lane = lax.broadcasted_iota(jnp.int32, (16, BLK), 1)
    res_ref[...] = jnp.where(lane == 0, sums[:16], sums[16:])


def on_device(loads, factor, pivots, lower, upper, incidence, counts):
    area_count, scenarios, order = loads.shape
    slots = incidence.shape[1]
    items = area_count * slots
    n_dev = lax.axis_size("dev")
    n_region = lax.axis_size("region")
    groups = n_dev + n_region
    peers = groups - 2
    table_rows = groups * BUS_DEV
    places = ROWS_SLOT * items
    rows = area_count * scenarios
    live_slot = jnp.arange(slots)[None, :] < counts[:, None]
    owner = incidence // BUS_DEV
    near = owner // n_dev == lax.axis_index("region")
    group = jnp.where(near, owner % n_dev, n_dev + owner // n_dev)
    at = jnp.where(live_slot, group * BUS_DEV + incidence % BUS_DEV, -1).astype(jnp.int32)

    vmem = pl.BlockSpec(memory_space=pltpu.VMEM)
    square = pltpu.VMEM((items, BLK), F32)
    bus = pltpu.VMEM((BUS_DEV, BLK), F32)
    listed = pltpu.VMEM((table_rows, BLK), F32)
    dma = pltpu.SemaphoreType.DMA
    dispatch, duals, res = pl.pallas_call(
        functools.partial(kernel, n_region, n_dev, area_count, scenarios, order, slots),
        out_shape=(
            jax.ShapeDtypeStruct(loads.shape, F32),
            jax.ShapeDtypeStruct((items, BLK), F32),
            jax.ShapeDtypeStruct((16, BLK), F32),
        ),
        in_specs=[vmem, pl.BlockSpec(memory_space=pl.ANY)] + [vmem] * 5,
        out_specs=(vmem, vmem, vmem),
        scratch_shapes=[
            pltpu.VMEM((area_count, order, order), BF16),
            pltpu.VMEM((order, places), BF16),
            pltpu.VMEM((rows, order), F32),
            pltpu.VMEM((rows, order), BF16),
            pltpu.VMEM((rows, order), F32),
            pltpu.VMEM((table_rows, items), BF16),
            pltpu.VMEM((items, table_rows), BF16),
            square, square, square, square, square, square, square, square, square,
            listed, listed, listed, bus, listed, bus,
            pltpu.VMEM((32, BLK), F32),
            pltpu.VMEM((n_dev, 32, BLK), F32),
            pltpu.VMEM((n_region, 32, BLK), F32),
            dma((area_count,)), dma((peers,)), dma((peers,)), dma((groups,)), dma((groups,)), dma((groups,)),
            dma((n_dev,)), dma((n_region,)),
        ],
        compiler_params=pltpu.CompilerParams(
            collective_id=0, has_side_effects=True, vmem_limit_bytes=48 * 1024 * 1024
        ),
        name="admm",
    )(loads, factor, pivots, lower, upper, at.reshape(1, items), at.reshape(items, 1))
    return dispatch, duals.reshape(area_count, slots, BLK), res[:ITERS, :2]


def solution(mesh):
    placed = (
        P(("region", "dev"), None, None),
        P(("region", "dev"), None, None),
        P(("region", "dev"), None),
        P(("region", "dev"), None),
        P(("region", "dev"), None),
        P(("region", "dev"), None),
        P(("region", "dev")),
    )
    return jax.shard_map(
        on_device,
        mesh=mesh,
        in_specs=placed,
        out_specs=(P(("region", "dev"), None, None), P(("region", "dev"), None, None), P()),
        check_vma=False,
    )
```

```python
import functools

import jax
import jax.numpy as jnp
from jax import lax
from jax.experimental import pallas as pl
from jax.experimental.pallas import tpu as pltpu
from jax.sharding import PartitionSpec as P

ROWS_SLOT = 4
BLK = 128
BUS_DEV = 16
ITERS = 14
RHO = 4.0
SIGMA = 1.0
TILE = 256
F32 = jnp.float32
BF16 = jnp.bfloat16
MESH = pl.DeviceIdType.MESH
NT = (((1,), (1,)), ((), ()))
NN = (((1,), (0,)), ((), ()))


def mm(left, right, dims=NN):
    return lax.dot_general(left, right, dims, preferred_element_type=F32)


def split3(x):
    high = x.astype(BF16)
    rest = x - high.astype(F32)
    mid = rest.astype(BF16)
    low = (rest - mid.astype(F32)).astype(BF16)
    return high, mid, low


def kernel(
    n_region, n_dev, area_count, scenarios, order, slots,
    loads_hbm, factor_ref, pivots_hbm, lower_hbm, upper_hbm, row_ref, col_ref,
    dispatch_ref, duals_ref, res_ref,
    loads_ref, pivots_ref, lower_ref, upper_ref, fac, wide, known, scaled, offset, pick, place, live, rhs_b, base_b, off_b, loads_b, low_b, up_b, blk, duals,
    part, got, table, mean, counts_got, members, res_sum, res_near, res_far,
    in_sem, fac_sem, send_sem, back_send, got_sem, table_sem, counts_sem, near_sem, far_sem,
):
    me_r = lax.axis_index("region")
    me_d = lax.axis_index("dev")
    items = area_count * slots
    rows = area_count * scenarios
    places = ROWS_SLOT * items
    edge = slots * ROWS_SLOT
    groups = n_dev + n_region
    near = [lax.rem(me_d + step, n_dev) for step in range(1, n_dev)]
    far = [lax.rem(me_r + step, n_region) for step in range(1, n_region)]
    peers = [((r, me_d), n_dev + r, n_dev + me_r, n_dev + r) for r in far]
    peers += [((me_r, d), d, me_d, d) for d in near]

    def factor_copy(area):
        return pltpu.make_async_copy(factor_ref.at[area], fac.at[area], fac_sem.at[area])

    inputs = [
        pltpu.make_async_copy(held, here, in_sem.at[number])
        for number, (held, here) in enumerate(
            ((loads_hbm, loads_ref), (pivots_hbm, pivots_ref), (lower_hbm, lower_ref), (upper_hbm, upper_ref))
        )
    ]
    for copy in inputs:
        copy.start()
    for area in range(area_count):
        factor_copy(area).start()

    got[...] = jnp.zeros_like(got)
    counts_got[...] = jnp.zeros_like(counts_got)
    table[...] = jnp.zeros_like(table)
    res_sum[...] = jnp.zeros_like(res_sum)

    barrier = pltpu.get_barrier_semaphore()
    for device, _, _, _ in peers:
        pl.semaphore_signal(barrier, inc=1, device_id=device, device_id_type=MESH)
    pl.semaphore_wait(barrier, len(peers))

    def group_rows(index):
        return pl.ds(pl.multiple_of(index * BUS_DEV, BUS_DEV), BUS_DEV)

    def outgoing(number, target, semaphores):
        device, theirs, mine, _ = peers[number]
        return pltpu.make_async_remote_copy(
            src_ref=part.at[group_rows(theirs)], dst_ref=target.at[group_rows(mine)],
            send_sem=send_sem.at[number], recv_sem=semaphores.at[mine],
            device_id=device, device_id_type=MESH,
        )

    def incoming(number, target, semaphores):
        device, theirs, _, here = peers[number]
        return pltpu.make_async_remote_copy(
            src_ref=part.at[group_rows(theirs)], dst_ref=target.at[group_rows(here)],
            send_sem=send_sem.at[number], recv_sem=semaphores.at[here],
            device_id=device, device_id_type=MESH,
        )

    def back(number, here=False):
        device, _, mine, theirs = peers[number]
        at = theirs if here else mine
        return pltpu.make_async_remote_copy(
            src_ref=mean, dst_ref=table.at[group_rows(at)],
            send_sem=back_send.at[number], recv_sem=table_sem.at[at],
            device_id=device, device_id_type=MESH,
        )

    def group_sum(ref):
        total = ref[0:BUS_DEV, :]
        for index in range(1, groups):
            total = total + ref[index * BUS_DEV : (index + 1) * BUS_DEV, :]
        return total

    picked = lax.broadcasted_iota(jnp.int32, (groups * BUS_DEV, items), 0) == row_ref[...]
    picked = jnp.where(picked, 1.0, 0.0)
    part[...] = jnp.broadcast_to(jnp.sum(picked, axis=1, keepdims=True), part.shape)
    for number in range(len(peers)):
        outgoing(number, counts_got, counts_sem).start()
    pick[...] = picked.astype(BF16)
    placed = lax.broadcasted_iota(jnp.int32, (items, groups * BUS_DEV), 1) == col_ref[...]
    place[...] = jnp.where(placed, 1.0, 0.0).astype(BF16)
    live[...] = jnp.broadcast_to(jnp.where(col_ref[...] >= 0, 1.0, 0.0), live.shape)
    counts_got[group_rows(me_d), :] = part[group_rows(me_d), :]

    source = lax.broadcasted_iota(jnp.int32, (area_count * BLK, places), 0)
    target = lax.broadcasted_iota(jnp.int32, (area_count * BLK, places), 1)
    slot_of = lax.rem(target, slots)
    area_of = lax.rem(target // slots, area_count)
    row_of = target // items
    order_hot = jnp.where(source == area_of * BLK + slot_of * ROWS_SLOT + row_of, 1.0, 0.0).astype(BF16)

    def stack_rows(x):
        return jnp.concatenate([x[:, r * items : (r + 1) * items] for r in range(ROWS_SLOT)], axis=0)

    def to_blocks(x):
        parts = [mm(piece, order_hot) for piece in split3(x)]
        return stack_rows(parts[0] + parts[1] + parts[2]).T

    for copy in inputs:
        copy.wait()
    loads_b[...] = to_blocks(jnp.concatenate([loads_ref[a, :, :BLK] for a in range(area_count)], axis=1))
    for bound, kept in ((lower_ref, low_b), (upper_ref, up_b)):
        line = jnp.concatenate([bound[a : a + 1, :BLK] for a in range(area_count)], axis=1)
        kept[...] = to_blocks(jnp.broadcast_to(line, (scenarios, area_count * BLK)))

    column = lax.broadcasted_iota(jnp.int32, (scenarios, TILE), 1)
    tiles = order // TILE

    def forward_known(area, pieces):
        at = slice(area * scenarios, (area + 1) * scenarios)
        for c in range(tiles):
            here = jnp.concatenate(pieces[: c + 1], axis=1) if c else pieces[0]
            known[at, c * TILE : (c + 1) * TILE] = mm(
                here, fac[area, c * TILE : (c + 1) * TILE, : (c + 1) * TILE], NT
            )

    def first(area):
        factor_copy(area).wait()
        pieces = []
        for c in range(tiles):
            value = loads_ref[area, :, c * TILE : (c + 1) * TILE]
            if c == 0:
                value = jnp.where(column < edge, 0.0, value)
            pieces.append(value.astype(BF16))
        forward_known(area, pieces)

    for area in range(area_count):
        first(area)

    def gather_wide(chunk, carry):
        at = pl.ds(pl.multiple_of(chunk * TILE, TILE), TILE)
        joined = jnp.concatenate([fac[a, at, :BLK] for a in range(area_count)], axis=1)
        wide[at, :] = mm(joined, order_hot).astype(BF16)
        return carry

    lax.fori_loop(0, tiles, gather_wide, 0)

    offset[...] = jnp.zeros_like(offset)
    off_b[...] = jnp.zeros_like(off_b)
    duals[...] = jnp.zeros_like(duals)
    mean[...] = jnp.zeros_like(mean)
    rhs_b[...] = loads_b[...]

    for number in range(len(peers)):
        incoming(number, counts_got, counts_sem).wait_recv()
        outgoing(number, counts_got, counts_sem).wait_send()
    members[...] = jnp.maximum(group_sum(counts_got), 1.0)

    own_area = lax.broadcasted_iota(jnp.int32, (scenarios, places), 1)
    own_area = lax.rem(own_area // slots, area_count)

    def dispatch_of(area):
        at = slice(area * scenarios, (area + 1) * scenarios)
        pieces = []
        for c in range(tiles):
            cols = slice(c * TILE, (c + 1) * TILE)
            found = mm(scaled[at, c * TILE :], fac[area, c * TILE :, cols])
            dispatch_ref[area, :, cols] = found
            moved = found + offset[at, cols]
            boxed = jnp.clip(moved, lower_ref[area : area + 1, cols], upper_ref[area : area + 1, cols])
            rest = moved - boxed
            offset[at, cols] = rest
            value = loads_ref[area, :, cols] + SIGMA * (boxed - rest)
            if c == 0:
                value = jnp.where(column < edge, 0.0, value)
            pieces.append(value.astype(BF16))
        return pieces

    def interior(begin, finish):
        waiting = dispatch_of(begin)
        for area in range(begin, finish):
            after = dispatch_of(area + 1) if area + 1 < finish else None
            forward_known(area, waiting)
            waiting = after

    def iterate(step, carry):
        turned = rhs_b[...].T
        flat = jnp.concatenate(
            [turned[r * scenarios : (r + 1) * scenarios, :] for r in range(ROWS_SLOT)], axis=1
        )
        left = jnp.concatenate(
            [jnp.where(own_area == a, flat, 0.0) for a in range(area_count)], axis=0
        ).astype(BF16)
        for c in range(tiles):
            cols = slice(c * TILE, (c + 1) * TILE)
            forward = known[:, cols] + mm(left, wide[cols, :], NT)
            forward = forward.reshape(area_count, scenarios, TILE) * pivots_ref[:, cols][:, None, :]
            scaled[:, cols] = forward.reshape(rows, TILE).astype(BF16)
        product = mm(scaled[...], wide[...])
        total = jnp.zeros((scenarios, places), F32)
        for a in range(area_count):
            total = total + jnp.where(own_area == a, product[a * scenarios : (a + 1) * scenarios, :], 0.0)
        block = stack_rows(total).T
        blk[...] = block
        values = (block + duals[...]) * live[...]
        pieces = split3(values)
        part[...] = mm(pick[...], pieces[0]) + mm(pick[...], pieces[1]) + mm(pick[...], pieces[2])
        for number in range(len(peers)):
            outgoing(number, got, got_sem).start()
        got[group_rows(me_d), :] = part[group_rows(me_d), :]
        moved = block + off_b[...]
        boxed = jnp.clip(moved, low_b[...], up_b[...])
        rest = moved - boxed
        off_b[...] = rest
        base_b[...] = loads_b[...] + SIGMA * (boxed - rest)

        interior(0, area_count // 2)

        for number in range(len(peers)):
            incoming(number, got, got_sem).wait_recv()
        fresh = group_sum(got) / members[...]
        change = fresh - mean[...]
        mean[...] = fresh
        for number in range(len(peers)):
            back(number).start()
        table[group_rows(me_d), :] = fresh
        res_sum[pl.ds(16 + step, 1), :] = (RHO * RHO) * jnp.sum(change * change, axis=0, keepdims=True)

        interior(area_count // 2, area_count)

        for number in range(len(peers)):
            back(number, here=True).wait_recv()
        pieces = split3(table[...])
        z_slot = mm(place[...], pieces[0]) + mm(place[...], pieces[1]) + mm(place[...], pieces[2])
        gap = (blk[...] - z_slot) * live[...]
        fresh_duals = duals[...] + gap
        duals[...] = fresh_duals
        rhs_b[...] = base_b[...] + RHO * (live[...] * (z_slot - fresh_duals))
        res_sum[pl.ds(step, 1), :] = jnp.sum(gap * gap, axis=0, keepdims=True)
        for number in range(len(peers)):
            outgoing(number, got, got_sem).wait_send()
            back(number).wait_send()
        return carry

    lax.fori_loop(0, ITERS, iterate, 0)

    def near_copy(number, here=False):
        device, _, mine, theirs = peers[number]
        at = theirs if here else mine
        return pltpu.make_async_remote_copy(
            src_ref=res_sum, dst_ref=res_near.at[at],
            send_sem=send_sem.at[number], recv_sem=near_sem.at[at], device_id=device, device_id_type=MESH,
        )

    def far_copy(number, here=False):
        device, _, mine, theirs = peers[number]
        at = (theirs if here else mine) - n_dev
        return pltpu.make_async_remote_copy(
            src_ref=res_sum, dst_ref=res_far.at[at],
            send_sem=send_sem.at[number], recv_sem=far_sem.at[at], device_id=device, device_id_type=MESH,
        )

    fars = range(n_region - 1)
    nears = range(n_region - 1, len(peers))
    for number in nears:
        near_copy(number).start()
    res_near[pl.ds(me_d, 1)] = res_sum[...][None]
    lane_from = lax.broadcasted_iota(jnp.int32, (BLK, BLK), 0)
    lane_to = lax.broadcasted_iota(jnp.int32, (BLK, BLK), 1)
    wanted = lax.rem(lane_to, ROWS_SLOT) * scenarios + lane_to // ROWS_SLOT
    lanes_hot = jnp.where(lane_from == wanted, 1.0, 0.0).astype(BF16)
    pieces = split3(duals[...])
    duals_ref[...] = mm(pieces[0], lanes_hot) + mm(pieces[1], lanes_hot) + mm(pieces[2], lanes_hot)
    for number in nears:
        near_copy(number, here=True).wait_recv()
        near_copy(number).wait_send()
    total = res_near[0]
    for index in range(1, n_dev):
        total = total + res_near[index]
    res_sum[...] = total
    for number in fars:
        far_copy(number).start()
    res_far[pl.ds(me_r, 1)] = total[None]
    for number in fars:
        far_copy(number, here=True).wait_recv()
        far_copy(number).wait_send()
    total = res_far[0]
    for index in range(1, n_region):
        total = total + res_far[index]
    sums = jnp.sum(total, axis=1, keepdims=True) / float(area_count * n_dev * n_region * BLK)
    lane = lax.broadcasted_iota(jnp.int32, (16, BLK), 1)
    res_ref[...] = jnp.where(lane == 0, sums[:16], sums[16:])


def on_device(loads, factor, pivots, lower, upper, incidence, counts):
    area_count, scenarios, order = loads.shape
    slots = incidence.shape[1]
    items = area_count * slots
    n_dev = lax.axis_size("dev")
    n_region = lax.axis_size("region")
    groups = n_dev + n_region
    peers = groups - 2
    table_rows = groups * BUS_DEV
    places = ROWS_SLOT * items
    rows = area_count * scenarios
    live_slot = jnp.arange(slots)[None, :] < counts[:, None]
    owner = incidence // BUS_DEV
    near = owner // n_dev == lax.axis_index("region")
    group = jnp.where(near, owner % n_dev, n_dev + owner // n_dev)
    at = jnp.where(live_slot, group * BUS_DEV + incidence % BUS_DEV, -1).astype(jnp.int32)

    vmem = pl.BlockSpec(memory_space=pltpu.VMEM)
    square = pltpu.VMEM((items, BLK), F32)
    bus = pltpu.VMEM((BUS_DEV, BLK), F32)
    listed = pltpu.VMEM((table_rows, BLK), F32)
    dma = pltpu.SemaphoreType.DMA
    dispatch, duals, res = pl.pallas_call(
        functools.partial(kernel, n_region, n_dev, area_count, scenarios, order, slots),
        out_shape=(
            jax.ShapeDtypeStruct(loads.shape, F32),
            jax.ShapeDtypeStruct((items, BLK), F32),
            jax.ShapeDtypeStruct((16, BLK), F32),
        ),
        in_specs=[pl.BlockSpec(memory_space=pl.ANY)] * 5 + [vmem] * 2,
        out_specs=(vmem, vmem, vmem),
        scratch_shapes=[
            pltpu.VMEM(loads.shape, F32),
            pltpu.VMEM(pivots.shape, F32),
            pltpu.VMEM(lower.shape, F32),
            pltpu.VMEM(upper.shape, F32),
            pltpu.VMEM((area_count, order, order), BF16),
            pltpu.VMEM((order, places), BF16),
            pltpu.VMEM((rows, order), F32),
            pltpu.VMEM((rows, order), BF16),
            pltpu.VMEM((rows, order), F32),
            pltpu.VMEM((table_rows, items), BF16),
            pltpu.VMEM((items, table_rows), BF16),
            square, square, square, square, square, square, square, square, square,
            listed, listed, listed, bus, listed, bus,
            pltpu.VMEM((32, BLK), F32),
            pltpu.VMEM((n_dev, 32, BLK), F32),
            pltpu.VMEM((n_region, 32, BLK), F32),
            dma((4,)), dma((area_count,)), dma((peers,)), dma((peers,)), dma((groups,)), dma((groups,)), dma((groups,)),
            dma((n_dev,)), dma((n_region,)),
        ],
        compiler_params=pltpu.CompilerParams(
            collective_id=0, has_side_effects=True, vmem_limit_bytes=60 * 1024 * 1024
        ),
        name="admm",
    )(loads, factor, pivots, lower, upper, at.reshape(1, items), at.reshape(items, 1))
    return dispatch, duals.reshape(area_count, slots, BLK), res[:ITERS, :2]


def solution(mesh):
    placed = (
        P(("region", "dev"), None, None),
        P(("region", "dev"), None, None),
        P(("region", "dev"), None),
        P(("region", "dev"), None),
        P(("region", "dev"), None),
        P(("region", "dev"), None),
        P(("region", "dev")),
    )
    return jax.shard_map(
        on_device,
        mesh=mesh,
        in_specs=placed,
        out_specs=(P(("region", "dev"), None, None), P(("region", "dev"), None, None), P()),
        check_vma=False,
    )
```

```python
import functools

import jax
import jax.numpy as jnp
from jax import lax
from jax.experimental import pallas as pl
from jax.experimental.pallas import tpu as pltpu
from jax.sharding import PartitionSpec as P

ROWS_SLOT = 4
BLK = 128
BUS_DEV = 16
ITERS = 14
RHO = 4.0
SIGMA = 1.0
TILE = 256
F32 = jnp.float32
BF16 = jnp.bfloat16
MESH = pl.DeviceIdType.MESH
NT = (((1,), (1,)), ((), ()))
NN = (((1,), (0,)), ((), ()))


def mm(left, right, dims=NN):
    return lax.dot_general(left, right, dims, preferred_element_type=F32)


def split3(x):
    high = x.astype(BF16)
    rest = x - high.astype(F32)
    mid = rest.astype(BF16)
    low = (rest - mid.astype(F32)).astype(BF16)
    return high, mid, low


def kernel(
    n_region, n_dev, area_count, scenarios, order, slots,
    loads_hbm, factor_ref, pivots_hbm, lower_hbm, upper_hbm, row_ref, col_ref,
    dispatch_ref, duals_ref, res_ref,
    loads_ref, pivots_ref, lower_ref, upper_ref, fac, gram, turned_fac, diag, wide, edges, hot, known, known_b, diag_b, rounded, offset,
    pick, place, live, rhs_b, base_b, off_b, loads_b, low_b, up_b, blk, duals,
    part, got, table, mean, counts_got, members, res_sum, res_near, res_far,
    in_sem, fac_sem, send_sem, back_send, got_sem, table_sem, counts_sem, near_sem, far_sem,
):
    me_r = lax.axis_index("region")
    me_d = lax.axis_index("dev")
    items = area_count * slots
    rows = area_count * scenarios
    places = ROWS_SLOT * items
    edge = slots * ROWS_SLOT
    groups = n_dev + n_region
    near = [lax.rem(me_d + step, n_dev) for step in range(1, n_dev)]
    far = [lax.rem(me_r + step, n_region) for step in range(1, n_region)]
    peers = [((r, me_d), n_dev + r, n_dev + me_r, n_dev + r) for r in far]
    peers += [((me_r, d), d, me_d, d) for d in near]

    def factor_copy(area):
        return pltpu.make_async_copy(factor_ref.at[area], fac.at[area], fac_sem.at[area])

    inputs = [
        pltpu.make_async_copy(held, here, in_sem.at[number])
        for number, (held, here) in enumerate(
            ((loads_hbm, loads_ref), (pivots_hbm, pivots_ref), (lower_hbm, lower_ref), (upper_hbm, upper_ref))
        )
    ]
    for copy in inputs:
        copy.start()
    for area in range(area_count):
        factor_copy(area).start()

    got[...] = jnp.zeros_like(got)
    counts_got[...] = jnp.zeros_like(counts_got)
    table[...] = jnp.zeros_like(table)
    res_sum[...] = jnp.zeros_like(res_sum)

    barrier = pltpu.get_barrier_semaphore()
    for device, _, _, _ in peers:
        pl.semaphore_signal(barrier, inc=1, device_id=device, device_id_type=MESH)
    pl.semaphore_wait(barrier, len(peers))

    def group_rows(index):
        return pl.ds(pl.multiple_of(index * BUS_DEV, BUS_DEV), BUS_DEV)

    def outgoing(number, target, semaphores):
        device, theirs, mine, _ = peers[number]
        return pltpu.make_async_remote_copy(
            src_ref=part.at[group_rows(theirs)], dst_ref=target.at[group_rows(mine)],
            send_sem=send_sem.at[number], recv_sem=semaphores.at[mine],
            device_id=device, device_id_type=MESH,
        )

    def incoming(number, target, semaphores):
        device, theirs, _, here = peers[number]
        return pltpu.make_async_remote_copy(
            src_ref=part.at[group_rows(theirs)], dst_ref=target.at[group_rows(here)],
            send_sem=send_sem.at[number], recv_sem=semaphores.at[here],
            device_id=device, device_id_type=MESH,
        )

    def back(number, here=False):
        device, _, mine, theirs = peers[number]
        at = theirs if here else mine
        return pltpu.make_async_remote_copy(
            src_ref=mean, dst_ref=table.at[group_rows(at)],
            send_sem=back_send.at[number], recv_sem=table_sem.at[at],
            device_id=device, device_id_type=MESH,
        )

    def group_sum(ref):
        total = ref[0:BUS_DEV, :]
        for index in range(1, groups):
            total = total + ref[index * BUS_DEV : (index + 1) * BUS_DEV, :]
        return total

    picked = lax.broadcasted_iota(jnp.int32, (groups * BUS_DEV, items), 0) == row_ref[...]
    picked = jnp.where(picked, 1.0, 0.0)
    part[...] = jnp.broadcast_to(jnp.sum(picked, axis=1, keepdims=True), part.shape)
    for number in range(len(peers)):
        outgoing(number, counts_got, counts_sem).start()
    pick[...] = picked.astype(BF16)
    placed = lax.broadcasted_iota(jnp.int32, (items, groups * BUS_DEV), 1) == col_ref[...]
    place[...] = jnp.where(placed, 1.0, 0.0).astype(BF16)
    live[...] = jnp.broadcast_to(jnp.where(col_ref[...] >= 0, 1.0, 0.0), live.shape)
    counts_got[group_rows(me_d), :] = part[group_rows(me_d), :]

    def place_of(index):
        return lax.rem(index // slots, area_count), lax.rem(index, slots) * ROWS_SLOT + index // items

    source = lax.broadcasted_iota(jnp.int32, (area_count * BLK, places), 0)
    area_of, column_of = place_of(lax.broadcasted_iota(jnp.int32, (area_count * BLK, places), 1))
    hot[...] = jnp.where(source == area_of * BLK + column_of, 1.0, 0.0).astype(BF16)

    def stack_rows(x):
        return jnp.concatenate([x[:, r * items : (r + 1) * items] for r in range(ROWS_SLOT)], axis=0)

    def to_flat(x):
        parts = mm(jnp.concatenate(split3(x), axis=0), hot[...])
        return parts[:scenarios] + parts[scenarios : 2 * scenarios] + parts[2 * scenarios :]

    def line_flat(ref):
        line = jnp.concatenate([ref[a : a + 1, :BLK] for a in range(area_count)], axis=1)
        return to_flat(jnp.broadcast_to(line, (scenarios, area_count * BLK)))

    for copy in inputs:
        copy.wait()
    loads_b[...] = stack_rows(
        to_flat(jnp.concatenate([loads_ref[a, :, :BLK] for a in range(area_count)], axis=1))
    ).T
    low_b[...] = stack_rows(line_flat(lower_ref)).T
    up_b[...] = stack_rows(line_flat(upper_ref)).T

    tiles = order // TILE
    column = lax.broadcasted_iota(jnp.int32, (1, TILE), 1)
    cut = [slice(c * TILE, (c + 1) * TILE) for c in range(tiles)]

    for c in range(tiles):
        value = loads_ref[:, :, cut[c]].reshape(rows, TILE)
        if c == 0:
            value = jnp.where(column < edge, 0.0, value)
        rounded[:, cut[c]] = value.astype(BF16)

    same = lax.broadcasted_iota(jnp.int32, (TILE, TILE), 0) == lax.broadcasted_iota(jnp.int32, (TILE, TILE), 1)
    unit = jnp.where(same, 1.0, 0.0).astype(BF16)

    def form(area, carry):
        factor_copy(area).wait()
        pivot = pivots_ref[pl.ds(area, 1), :]
        for k in range(tiles):
            for i in range(k, tiles):
                flipped = mm(unit, fac[area, cut[i], cut[k]], NT)
                turned_fac[cut[k], cut[i]] = (flipped * pivot[:, cut[i]]).astype(BF16)
        for k in range(tiles):
            for n in range(tiles):
                begin = max(k, n) * TILE
                value = mm(turned_fac[cut[k], begin:], fac[area, begin:, cut[n]])
                if k == n:
                    exact = pivot[:, cut[k]]
                    found = jnp.sum(jnp.where(same, value, 0.0), axis=0, keepdims=True)
                    diag[pl.ds(area, 1), cut[k]] = found - exact.astype(BF16).astype(F32) + exact
                    value = jnp.where(same, 0.0, value)
                gram[area, cut[k], cut[n]] = value.astype(BF16)
        return carry

    lax.fori_loop(0, area_count, form, 0)

    target = lax.broadcasted_iota(jnp.int32, (places, area_count * BLK), 1)
    area_of, column_of = place_of(lax.broadcasted_iota(jnp.int32, (places, area_count * BLK), 0))
    hot_rows = jnp.where(target == area_of * BLK + column_of, 1.0, 0.0).astype(BF16)
    for c in range(tiles):
        joined = jnp.concatenate([gram[a, :BLK, cut[c]] for a in range(area_count)], axis=0)
        wide[:, cut[c]] = mm(hot_rows, joined).astype(BF16)
    source = lax.broadcasted_iota(jnp.int32, (BLK, places), 0)
    _, column_of = place_of(lax.broadcasted_iota(jnp.int32, (BLK, places), 1))
    spread = jnp.where(source == column_of, 1.0, 0.0).astype(BF16)
    area_left, _ = place_of(lax.broadcasted_iota(jnp.int32, (places, places), 0))
    area_right, _ = place_of(lax.broadcasted_iota(jnp.int32, (places, places), 1))
    edges[...] = jnp.where(area_left == area_right, mm(wide[:, :BLK], spread), 0.0).astype(BF16)
    diag_b[...] = line_flat(diag)

    offset[...] = jnp.zeros_like(offset)
    off_b[...] = jnp.zeros_like(off_b)
    duals[...] = jnp.zeros_like(duals)
    mean[...] = jnp.zeros_like(mean)
    rhs_b[...] = loads_b[...]

    for number in range(len(peers)):
        incoming(number, counts_got, counts_sem).wait_recv()
        outgoing(number, counts_got, counts_sem).wait_send()
    members[...] = jnp.maximum(group_sum(counts_got), 1.0)

    own_area, _ = place_of(lax.broadcasted_iota(jnp.int32, (scenarios, places), 1))

    def product(area, carry):
        at = pl.ds(pl.multiple_of(area * scenarios, scenarios), scenarios)
        for c in range(tiles):
            straight = rounded[at, cut[c]].astype(F32) * diag[pl.ds(area, 1), cut[c]]
            known[at, cut[c]] = mm(rounded[at, :], gram[area, :, cut[c]]) + straight
        return carry

    def known_edges():
        joined = [known[a * scenarios : (a + 1) * scenarios, :BLK] for a in range(area_count)]
        known_b[...] = to_flat(jnp.concatenate(joined, axis=1))

    lax.fori_loop(0, area_count, product, 0)
    known_edges()

    _, column_of = place_of(lax.broadcasted_iota(jnp.int32, (places, TILE), 0))
    back_hot = lax.broadcasted_iota(jnp.int32, (places, TILE), 1) == column_of
    back_hot = jnp.where(back_hot, 1.0, 0.0).astype(BF16)

    def iterate(step, carry):
        turned = rhs_b[...].T
        flat = jnp.concatenate(
            [turned[r * scenarios : (r + 1) * scenarios, :] for r in range(ROWS_SLOT)], axis=1
        )
        flat = flat.astype(BF16)
        solved = known_b[...] + mm(flat, edges[...]) + flat.astype(F32) * diag_b[...]
        block = stack_rows(solved).T
        blk[...] = block
        values = (block + duals[...]) * live[...]
        pieces = split3(values)
        part[...] = mm(pick[...], pieces[0]) + mm(pick[...], pieces[1]) + mm(pick[...], pieces[2])
        for number in range(len(peers)):
            outgoing(number, got, got_sem).start()
        got[group_rows(me_d), :] = part[group_rows(me_d), :]
        moved = block + off_b[...]
        boxed = jnp.clip(moved, low_b[...], up_b[...])
        rest = moved - boxed
        off_b[...] = rest
        base_b[...] = loads_b[...] + SIGMA * (boxed - rest)

        left = jnp.concatenate(
            [jnp.where(own_area == a, flat.astype(F32), 0.0) for a in range(area_count)], axis=0
        ).astype(BF16)
        for c in range(tiles):
            found = known[:, cut[c]] + mm(left, wide[:, cut[c]])
            found = found.reshape(area_count, scenarios, TILE)
            if c == 0:
                natural = mm(left, back_hot).reshape(area_count, scenarios, TILE)
                found = found + natural * diag[:, cut[c]][:, None, :]
            dispatch_ref[:, :, cut[c]] = found
            moved = found + offset[:, :, cut[c]]
            boxed = jnp.clip(moved, lower_ref[:, cut[c]][:, None, :], upper_ref[:, cut[c]][:, None, :])
            rest = moved - boxed
            offset[:, :, cut[c]] = rest
            value = (loads_ref[:, :, cut[c]] + SIGMA * (boxed - rest)).reshape(rows, TILE)
            if c == 0:
                value = jnp.where(column < edge, 0.0, value)
            rounded[:, cut[c]] = value.astype(BF16)

        more = step < ITERS - 1

        @pl.when(more)
        def _():
            lax.fori_loop(0, area_count // 2, product, 0)

        for number in range(len(peers)):
            incoming(number, got, got_sem).wait_recv()
        fresh = group_sum(got) / members[...]
        change = fresh - mean[...]
        mean[...] = fresh
        for number in range(len(peers)):
            back(number).start()
        table[group_rows(me_d), :] = fresh
        res_sum[pl.ds(16 + step, 1), :] = (RHO * RHO) * jnp.sum(change * change, axis=0, keepdims=True)

        @pl.when(more)
        def _():
            lax.fori_loop(area_count // 2, area_count, product, 0)
            known_edges()

        for number in range(len(peers)):
            back(number, here=True).wait_recv()
        pieces = split3(table[...])
        z_slot = mm(place[...], pieces[0]) + mm(place[...], pieces[1]) + mm(place[...], pieces[2])
        gap = (blk[...] - z_slot) * live[...]
        fresh_duals = duals[...] + gap
        duals[...] = fresh_duals
        rhs_b[...] = base_b[...] + RHO * (live[...] * (z_slot - fresh_duals))
        res_sum[pl.ds(step, 1), :] = jnp.sum(gap * gap, axis=0, keepdims=True)
        for number in range(len(peers)):
            outgoing(number, got, got_sem).wait_send()
            back(number).wait_send()
        return carry

    lax.fori_loop(0, ITERS, iterate, 0)

    def near_copy(number, here=False):
        device, _, mine, theirs = peers[number]
        at = theirs if here else mine
        return pltpu.make_async_remote_copy(
            src_ref=res_sum, dst_ref=res_near.at[at],
            send_sem=send_sem.at[number], recv_sem=near_sem.at[at], device_id=device, device_id_type=MESH,
        )

    def far_copy(number, here=False):
        device, _, mine, theirs = peers[number]
        at = (theirs if here else mine) - n_dev
        return pltpu.make_async_remote_copy(
            src_ref=res_sum, dst_ref=res_far.at[at],
            send_sem=send_sem.at[number], recv_sem=far_sem.at[at], device_id=device, device_id_type=MESH,
        )

    fars = range(n_region - 1)
    nears = range(n_region - 1, len(peers))
    for number in nears:
        near_copy(number).start()
    res_near[pl.ds(me_d, 1)] = res_sum[...][None]
    lane_from = lax.broadcasted_iota(jnp.int32, (BLK, BLK), 0)
    lane_to = lax.broadcasted_iota(jnp.int32, (BLK, BLK), 1)
    wanted = lax.rem(lane_to, ROWS_SLOT) * scenarios + lane_to // ROWS_SLOT
    lanes_hot = jnp.where(lane_from == wanted, 1.0, 0.0).astype(BF16)
    pieces = split3(duals[...])
    duals_ref[...] = mm(pieces[0], lanes_hot) + mm(pieces[1], lanes_hot) + mm(pieces[2], lanes_hot)
    for number in nears:
        near_copy(number, here=True).wait_recv()
        near_copy(number).wait_send()
    total = res_near[0]
    for index in range(1, n_dev):
        total = total + res_near[index]
    res_sum[...] = total
    for number in fars:
        far_copy(number).start()
    res_far[pl.ds(me_r, 1)] = total[None]
    for number in fars:
        far_copy(number, here=True).wait_recv()
        far_copy(number).wait_send()
    total = res_far[0]
    for index in range(1, n_region):
        total = total + res_far[index]
    sums = jnp.sum(total, axis=1, keepdims=True) / float(area_count * n_dev * n_region * BLK)
    lane = lax.broadcasted_iota(jnp.int32, (16, BLK), 1)
    res_ref[...] = jnp.where(lane == 0, sums[:16], sums[16:])


def on_device(loads, factor, pivots, lower, upper, incidence, counts):
    area_count, scenarios, order = loads.shape
    slots = incidence.shape[1]
    items = area_count * slots
    n_dev = lax.axis_size("dev")
    n_region = lax.axis_size("region")
    groups = n_dev + n_region
    peers = groups - 2
    table_rows = groups * BUS_DEV
    places = ROWS_SLOT * items
    rows = area_count * scenarios
    live_slot = jnp.arange(slots)[None, :] < counts[:, None]
    owner = incidence // BUS_DEV
    near = owner // n_dev == lax.axis_index("region")
    group = jnp.where(near, owner % n_dev, n_dev + owner // n_dev)
    at = jnp.where(live_slot, group * BUS_DEV + incidence % BUS_DEV, -1).astype(jnp.int32)

    vmem = pl.BlockSpec(memory_space=pltpu.VMEM)
    square = pltpu.VMEM((items, BLK), F32)
    bus = pltpu.VMEM((BUS_DEV, BLK), F32)
    listed = pltpu.VMEM((table_rows, BLK), F32)
    dma = pltpu.SemaphoreType.DMA
    dispatch, duals, res = pl.pallas_call(
        functools.partial(kernel, n_region, n_dev, area_count, scenarios, order, slots),
        out_shape=(
            jax.ShapeDtypeStruct(loads.shape, F32),
            jax.ShapeDtypeStruct((items, BLK), F32),
            jax.ShapeDtypeStruct((16, BLK), F32),
        ),
        in_specs=[pl.BlockSpec(memory_space=pl.ANY)] * 5 + [vmem] * 2,
        out_specs=(vmem, vmem, vmem),
        scratch_shapes=[
            pltpu.VMEM(loads.shape, F32),
            pltpu.VMEM(pivots.shape, F32),
            pltpu.VMEM(lower.shape, F32),
            pltpu.VMEM(upper.shape, F32),
            pltpu.VMEM((area_count, order, order), BF16),
            pltpu.VMEM((area_count, order, order), BF16),
            pltpu.VMEM((order, order), BF16),
            pltpu.VMEM((area_count, order), F32),
            pltpu.VMEM((places, order), BF16),
            pltpu.VMEM((places, places), BF16),
            pltpu.VMEM((area_count * BLK, places), BF16),
            pltpu.VMEM((rows, order), F32),
            pltpu.VMEM((scenarios, places), F32),
            pltpu.VMEM((scenarios, places), F32),
            pltpu.VMEM((rows, order), BF16),
            pltpu.VMEM(loads.shape, F32),
            pltpu.VMEM((table_rows, items), BF16),
            pltpu.VMEM((items, table_rows), BF16),
            square, square, square, square, square, square, square, square, square,
            listed, listed, listed, bus, listed, bus,
            pltpu.VMEM((32, BLK), F32),
            pltpu.VMEM((n_dev, 32, BLK), F32),
            pltpu.VMEM((n_region, 32, BLK), F32),
            dma((4,)), dma((area_count,)), dma((peers,)), dma((peers,)), dma((groups,)), dma((groups,)), dma((groups,)),
            dma((n_dev,)), dma((n_region,)),
        ],
        compiler_params=pltpu.CompilerParams(
            collective_id=0, has_side_effects=True, vmem_limit_bytes=60 * 1024 * 1024
        ),
        name="admm",
    )(loads, factor, pivots, lower, upper, at.reshape(1, items), at.reshape(items, 1))
    return dispatch, duals.reshape(area_count, slots, BLK), res[:ITERS, :2]


def solution(mesh):
    placed = (
        P(("region", "dev"), None, None),
        P(("region", "dev"), None, None),
        P(("region", "dev"), None),
        P(("region", "dev"), None),
        P(("region", "dev"), None),
        P(("region", "dev"), None),
        P(("region", "dev")),
    )
    return jax.shard_map(
        on_device,
        mesh=mesh,
        in_specs=placed,
        out_specs=(P(("region", "dev"), None, None), P(("region", "dev"), None, None), P()),
        check_vma=False,
    )
```

```python
import functools

import jax
import jax.numpy as jnp
from jax import lax
from jax.experimental import pallas as pl
from jax.experimental.pallas import tpu as pltpu
from jax.sharding import PartitionSpec as P

ROWS_SLOT = 4
BLK = 128
BUS_DEV = 16
ITERS = 14
RHO = 4.0
SIGMA = 1.0
TILE = 256
F32 = jnp.float32
BF16 = jnp.bfloat16
MESH = pl.DeviceIdType.MESH
NT = (((1,), (1,)), ((), ()))
NN = (((1,), (0,)), ((), ()))


def mm(left, right, dims=NN):
    return lax.dot_general(left, right, dims, preferred_element_type=F32)


def split3(x):
    high = x.astype(BF16)
    rest = x - high.astype(F32)
    mid = rest.astype(BF16)
    low = (rest - mid.astype(F32)).astype(BF16)
    return high, mid, low


def kernel(
    n_region, n_dev, area_count, scenarios, order, slots,
    loads_hbm, factor_ref, pivots_hbm, lower_hbm, upper_hbm, row_ref, col_ref,
    dispatch_ref, duals_ref, res_ref,
    loads_ref, pivots_ref, lower_ref, upper_ref, fac, gram, diag, wide, edges, hot, known, known_b, diag_b, rounded, offset,
    pick, place, live, rhs_b, base_b, off_b, loads_b, low_b, up_b, blk, duals,
    part, got, table, mean, counts_got, members, res_sum, res_near, res_far,
    in_sem, fac_sem, send_sem, back_send, got_sem, table_sem, counts_sem, near_sem, far_sem,
):
    me_r = lax.axis_index("region")
    me_d = lax.axis_index("dev")
    items = area_count * slots
    rows = area_count * scenarios
    places = ROWS_SLOT * items
    edge = slots * ROWS_SLOT
    groups = n_dev + n_region
    near = [lax.rem(me_d + step, n_dev) for step in range(1, n_dev)]
    far = [lax.rem(me_r + step, n_region) for step in range(1, n_region)]
    peers = [((r, me_d), n_dev + r, n_dev + me_r, n_dev + r) for r in far]
    peers += [((me_r, d), d, me_d, d) for d in near]

    def factor_copy(area):
        return pltpu.make_async_copy(factor_ref.at[area], fac.at[area], fac_sem.at[area])

    inputs = [
        pltpu.make_async_copy(held, here, in_sem.at[number])
        for number, (held, here) in enumerate(
            ((loads_hbm, loads_ref), (pivots_hbm, pivots_ref), (lower_hbm, lower_ref), (upper_hbm, upper_ref))
        )
    ]
    for copy in inputs:
        copy.start()
    for area in range(area_count):
        factor_copy(area).start()

    got[...] = jnp.zeros_like(got)
    counts_got[...] = jnp.zeros_like(counts_got)
    table[...] = jnp.zeros_like(table)
    res_sum[...] = jnp.zeros_like(res_sum)

    barrier = pltpu.get_barrier_semaphore()
    for device, _, _, _ in peers:
        pl.semaphore_signal(barrier, inc=1, device_id=device, device_id_type=MESH)
    pl.semaphore_wait(barrier, len(peers))

    def group_rows(index):
        return pl.ds(pl.multiple_of(index * BUS_DEV, BUS_DEV), BUS_DEV)

    def outgoing(number, target, semaphores):
        device, theirs, mine, _ = peers[number]
        return pltpu.make_async_remote_copy(
            src_ref=part.at[group_rows(theirs)], dst_ref=target.at[group_rows(mine)],
            send_sem=send_sem.at[number], recv_sem=semaphores.at[mine],
            device_id=device, device_id_type=MESH,
        )

    def incoming(number, target, semaphores):
        device, theirs, _, here = peers[number]
        return pltpu.make_async_remote_copy(
            src_ref=part.at[group_rows(theirs)], dst_ref=target.at[group_rows(here)],
            send_sem=send_sem.at[number], recv_sem=semaphores.at[here],
            device_id=device, device_id_type=MESH,
        )

    def back(number, here=False):
        device, _, mine, theirs = peers[number]
        at = theirs if here else mine
        return pltpu.make_async_remote_copy(
            src_ref=mean, dst_ref=table.at[group_rows(at)],
            send_sem=back_send.at[number], recv_sem=table_sem.at[at],
            device_id=device, device_id_type=MESH,
        )

    def group_sum(ref):
        total = ref[0:BUS_DEV, :]
        for index in range(1, groups):
            total = total + ref[index * BUS_DEV : (index + 1) * BUS_DEV, :]
        return total

    picked = lax.broadcasted_iota(jnp.int32, (groups * BUS_DEV, items), 0) == row_ref[...]
    picked = jnp.where(picked, 1.0, 0.0)
    part[...] = jnp.broadcast_to(jnp.sum(picked, axis=1, keepdims=True), part.shape)
    for number in range(len(peers)):
        outgoing(number, counts_got, counts_sem).start()
    pick[...] = picked.astype(BF16)
    placed = lax.broadcasted_iota(jnp.int32, (items, groups * BUS_DEV), 1) == col_ref[...]
    place[...] = jnp.where(placed, 1.0, 0.0).astype(BF16)
    live[...] = jnp.broadcast_to(jnp.where(row_ref[...] >= 0, 1.0, 0.0), live.shape)
    counts_got[group_rows(me_d), :] = part[group_rows(me_d), :]

    def place_of(index):
        return lax.rem(index // slots, area_count), lax.rem(index, slots) * ROWS_SLOT + index // items

    source = lax.broadcasted_iota(jnp.int32, (area_count * BLK, places), 0)
    area_of, column_of = place_of(lax.broadcasted_iota(jnp.int32, (area_count * BLK, places), 1))
    hot[...] = jnp.where(source == area_of * BLK + column_of, 1.0, 0.0).astype(BF16)

    def stack_rows(x):
        return jnp.concatenate([x[:, r * items : (r + 1) * items] for r in range(ROWS_SLOT)], axis=0)

    def to_flat(x):
        parts = mm(jnp.concatenate(split3(x), axis=0), hot[...])
        return parts[:scenarios] + parts[scenarios : 2 * scenarios] + parts[2 * scenarios :]

    def line_flat(ref):
        line = jnp.concatenate([ref[a : a + 1, :BLK] for a in range(area_count)], axis=1)
        return to_flat(jnp.broadcast_to(line, (scenarios, area_count * BLK)))

    for copy in inputs:
        copy.wait()
    loads_b[...] = stack_rows(
        to_flat(jnp.concatenate([loads_ref[a, :, :BLK] for a in range(area_count)], axis=1))
    )
    low_b[...] = stack_rows(line_flat(lower_ref))
    up_b[...] = stack_rows(line_flat(upper_ref))

    tiles = order // TILE
    column = lax.broadcasted_iota(jnp.int32, (1, TILE), 1)
    cut = [slice(c * TILE, (c + 1) * TILE) for c in range(tiles)]

    for c in range(tiles):
        value = loads_ref[:, :, cut[c]].reshape(rows, TILE)
        if c == 0:
            value = jnp.where(column < edge, 0.0, value)
        rounded[:, cut[c]] = value.astype(BF16)

    same = lax.broadcasted_iota(jnp.int32, (BLK, BLK), 0) == lax.broadcasted_iota(jnp.int32, (BLK, BLK), 1)
    unit = jnp.where(same, 1.0, 0.0).astype(BF16)

    def product(area, carry):
        at = pl.ds(pl.multiple_of(area * scenarios, scenarios), scenarios)
        scaled = []
        for c in range(tiles):
            end = (c + 1) * TILE
            forward = mm(rounded[at, :end], fac[area, cut[c], :end], NT)
            scaled.append((forward * pivots_ref[pl.ds(area, 1), cut[c]]).astype(BF16))
        scaled = jnp.concatenate(scaled, axis=1)
        for c in range(tiles):
            known[at, cut[c]] = mm(scaled[:, c * TILE :], fac[area, c * TILE :, cut[c]])
        return carry

    def form(area, carry):
        factor_copy(area).wait()
        pivot = pivots_ref[pl.ds(area, 1), :]
        flipped = (mm(unit, fac[area, :, :BLK], NT) * pivot).astype(BF16)
        for n in range(tiles):
            value = mm(flipped[:, n * TILE :], fac[area, n * TILE :, cut[n]])
            if n == 0:
                head = value[:, :BLK]
                exact = pivot[:, :BLK]
                found = jnp.sum(jnp.where(same, head, 0.0), axis=0, keepdims=True)
                diag[pl.ds(area, 1), :] = found - exact.astype(BF16).astype(F32) + exact
                value = jnp.concatenate([jnp.where(same, 0.0, head), value[:, BLK:]], axis=1)
            gram[area, :, cut[n]] = value.astype(BF16)
        product(area, carry)
        return carry

    lax.fori_loop(0, area_count, form, 0)

    target = lax.broadcasted_iota(jnp.int32, (places, area_count * BLK), 1)
    area_of, column_of = place_of(lax.broadcasted_iota(jnp.int32, (places, area_count * BLK), 0))
    hot_rows = jnp.where(target == area_of * BLK + column_of, 1.0, 0.0).astype(BF16)
    for c in range(tiles):
        joined = jnp.concatenate([gram[a, :, cut[c]] for a in range(area_count)], axis=0)
        wide[:, cut[c]] = mm(hot_rows, joined).astype(BF16)
    source = lax.broadcasted_iota(jnp.int32, (BLK, places), 0)
    _, column_of = place_of(lax.broadcasted_iota(jnp.int32, (BLK, places), 1))
    spread = jnp.where(source == column_of, 1.0, 0.0).astype(BF16)
    area_left, _ = place_of(lax.broadcasted_iota(jnp.int32, (places, places), 0))
    area_right, _ = place_of(lax.broadcasted_iota(jnp.int32, (places, places), 1))
    edges[...] = jnp.where(area_left == area_right, mm(wide[:, :BLK], spread), 0.0).astype(BF16)
    diag_b[...] = line_flat(diag)

    offset[...] = jnp.zeros_like(offset)
    off_b[...] = jnp.zeros_like(off_b)
    duals[...] = jnp.zeros_like(duals)
    mean[...] = jnp.zeros_like(mean)
    rhs_b[...] = loads_b[...]

    for number in range(len(peers)):
        incoming(number, counts_got, counts_sem).wait_recv()
        outgoing(number, counts_got, counts_sem).wait_send()
    members[...] = jnp.maximum(group_sum(counts_got), 1.0)

    own_area, _ = place_of(lax.broadcasted_iota(jnp.int32, (scenarios, places), 1))

    def known_edges():
        joined = [known[a * scenarios : (a + 1) * scenarios, :BLK] for a in range(area_count)]
        known_b[...] = to_flat(jnp.concatenate(joined, axis=1))

    known_edges()

    _, column_of = place_of(lax.broadcasted_iota(jnp.int32, (places, BLK), 0))
    back_hot = lax.broadcasted_iota(jnp.int32, (places, BLK), 1) == column_of
    back_hot = jnp.where(back_hot, 1.0, 0.0).astype(BF16)

    def iterate(step, carry):
        turned = rhs_b[...]
        flat = jnp.concatenate(
            [turned[r * scenarios : (r + 1) * scenarios, :] for r in range(ROWS_SLOT)], axis=1
        )
        flat = flat.astype(BF16)
        solved = known_b[...] + mm(flat, edges[...]) + flat.astype(F32) * diag_b[...]
        block = stack_rows(solved)
        blk[...] = block
        values = (block + duals[...]) * live[...]
        pieces = split3(values)
        part[...] = mm(pick[...], pieces[0], NT) + mm(pick[...], pieces[1], NT) + mm(pick[...], pieces[2], NT)
        for number in range(len(peers)):
            outgoing(number, got, got_sem).start()
        got[group_rows(me_d), :] = part[group_rows(me_d), :]
        moved = block + off_b[...]
        boxed = jnp.clip(moved, low_b[...], up_b[...])
        rest = moved - boxed
        off_b[...] = rest
        base_b[...] = loads_b[...] + SIGMA * (boxed - rest)

        left = jnp.concatenate(
            [jnp.where(own_area == a, flat.astype(F32), 0.0) for a in range(area_count)], axis=0
        ).astype(BF16)
        for c in range(tiles):
            found = known[:, cut[c]] + mm(left, wide[:, cut[c]])
            found = found.reshape(area_count, scenarios, TILE)
            if c == 0:
                natural = mm(left, back_hot).reshape(area_count, scenarios, BLK) * diag[...][:, None, :]
                found = jnp.concatenate([found[:, :, :BLK] + natural, found[:, :, BLK:]], axis=2)
            dispatch_ref[:, :, cut[c]] = found
            moved = found + offset[:, :, cut[c]]
            boxed = jnp.clip(moved, lower_ref[:, cut[c]][:, None, :], upper_ref[:, cut[c]][:, None, :])
            rest = moved - boxed
            offset[:, :, cut[c]] = rest
            value = (loads_ref[:, :, cut[c]] + SIGMA * (boxed - rest)).reshape(rows, TILE)
            if c == 0:
                value = jnp.where(column < edge, 0.0, value)
            rounded[:, cut[c]] = value.astype(BF16)

        more = step < ITERS - 1

        @pl.when(more)
        def _():
            lax.fori_loop(0, area_count // 2, product, 0)

        for number in range(len(peers)):
            incoming(number, got, got_sem).wait_recv()
        fresh = group_sum(got) / members[...]
        change = fresh - mean[...]
        mean[...] = fresh
        for number in range(len(peers)):
            back(number).start()
        table[group_rows(me_d), :] = fresh
        res_sum[pl.ds(16 + step, 1), :] = (RHO * RHO) * jnp.sum(change * change, axis=0, keepdims=True)

        @pl.when(more)
        def _():
            lax.fori_loop(area_count // 2, area_count, product, 0)
            known_edges()

        for number in range(len(peers)):
            back(number, here=True).wait_recv()
        pieces = split3(table[...])
        z_slot = (mm(place[...], pieces[0]) + mm(place[...], pieces[1]) + mm(place[...], pieces[2])).T
        gap = (blk[...] - z_slot) * live[...]
        fresh_duals = duals[...] + gap
        duals[...] = fresh_duals
        rhs_b[...] = base_b[...] + RHO * (live[...] * (z_slot - fresh_duals))
        res_sum[pl.ds(step, 1), :] = jnp.sum(gap * gap, axis=0, keepdims=True)
        for number in range(len(peers)):
            outgoing(number, got, got_sem).wait_send()
            back(number).wait_send()
        return carry

    lax.fori_loop(0, ITERS, iterate, 0)

    def near_copy(number, here=False):
        device, _, mine, theirs = peers[number]
        at = theirs if here else mine
        return pltpu.make_async_remote_copy(
            src_ref=res_sum, dst_ref=res_near.at[at],
            send_sem=send_sem.at[number], recv_sem=near_sem.at[at], device_id=device, device_id_type=MESH,
        )

    def far_copy(number, here=False):
        device, _, mine, theirs = peers[number]
        at = (theirs if here else mine) - n_dev
        return pltpu.make_async_remote_copy(
            src_ref=res_sum, dst_ref=res_far.at[at],
            send_sem=send_sem.at[number], recv_sem=far_sem.at[at], device_id=device, device_id_type=MESH,
        )

    fars = range(n_region - 1)
    nears = range(n_region - 1, len(peers))
    for number in nears:
        near_copy(number).start()
    res_near[pl.ds(me_d, 1)] = res_sum[...][None]
    lane_from = lax.broadcasted_iota(jnp.int32, (BLK, BLK), 0)
    lane_to = lax.broadcasted_iota(jnp.int32, (BLK, BLK), 1)
    wanted = lax.rem(lane_to, ROWS_SLOT) * scenarios + lane_to // ROWS_SLOT
    lanes_hot = jnp.where(lane_from == wanted, 1.0, 0.0).astype(BF16)
    pieces = split3(duals[...].T)
    duals_ref[...] = mm(pieces[0], lanes_hot) + mm(pieces[1], lanes_hot) + mm(pieces[2], lanes_hot)
    for number in nears:
        near_copy(number, here=True).wait_recv()
        near_copy(number).wait_send()
    total = res_near[0]
    for index in range(1, n_dev):
        total = total + res_near[index]
    res_sum[...] = total
    for number in fars:
        far_copy(number).start()
    res_far[pl.ds(me_r, 1)] = total[None]
    for number in fars:
        far_copy(number, here=True).wait_recv()
        far_copy(number).wait_send()
    total = res_far[0]
    for index in range(1, n_region):
        total = total + res_far[index]
    sums = jnp.sum(total, axis=1, keepdims=True) / float(area_count * n_dev * n_region * BLK)
    lane = lax.broadcasted_iota(jnp.int32, (16, BLK), 1)
    res_ref[...] = jnp.where(lane == 0, sums[:16], sums[16:])


def on_device(loads, factor, pivots, lower, upper, incidence, counts):
    area_count, scenarios, order = loads.shape
    slots = incidence.shape[1]
    items = area_count * slots
    n_dev = lax.axis_size("dev")
    n_region = lax.axis_size("region")
    groups = n_dev + n_region
    peers = groups - 2
    table_rows = groups * BUS_DEV
    places = ROWS_SLOT * items
    rows = area_count * scenarios
    live_slot = jnp.arange(slots)[None, :] < counts[:, None]
    owner = incidence // BUS_DEV
    near = owner // n_dev == lax.axis_index("region")
    group = jnp.where(near, owner % n_dev, n_dev + owner // n_dev)
    at = jnp.where(live_slot, group * BUS_DEV + incidence % BUS_DEV, -1).astype(jnp.int32)

    vmem = pl.BlockSpec(memory_space=pltpu.VMEM)
    square = pltpu.VMEM((items, BLK), F32)
    bus = pltpu.VMEM((BUS_DEV, BLK), F32)
    listed = pltpu.VMEM((table_rows, BLK), F32)
    dma = pltpu.SemaphoreType.DMA
    dispatch, duals, res = pl.pallas_call(
        functools.partial(kernel, n_region, n_dev, area_count, scenarios, order, slots),
        out_shape=(
            jax.ShapeDtypeStruct(loads.shape, F32),
            jax.ShapeDtypeStruct((items, BLK), F32),
            jax.ShapeDtypeStruct((16, BLK), F32),
        ),
        in_specs=[pl.BlockSpec(memory_space=pltpu.HBM)] * 5 + [vmem] * 2,
        out_specs=(vmem, vmem, vmem),
        scratch_shapes=[
            pltpu.VMEM(loads.shape, F32),
            pltpu.VMEM(pivots.shape, F32),
            pltpu.VMEM(lower.shape, F32),
            pltpu.VMEM(upper.shape, F32),
            pltpu.VMEM((area_count, order, order), BF16),
            pltpu.VMEM((area_count, BLK, order), BF16),
            pltpu.VMEM((area_count, BLK), F32),
            pltpu.VMEM((places, order), BF16),
            pltpu.VMEM((places, places), BF16),
            pltpu.VMEM((area_count * BLK, places), BF16),
            pltpu.VMEM((rows, order), F32),
            pltpu.VMEM((scenarios, places), F32),
            pltpu.VMEM((scenarios, places), F32),
            pltpu.VMEM((rows, order), BF16),
            pltpu.VMEM(loads.shape, F32),
            pltpu.VMEM((table_rows, items), BF16),
            pltpu.VMEM((items, table_rows), BF16),
            square, square, square, square, square, square, square, square, square,
            listed, listed, listed, bus, listed, bus,
            pltpu.VMEM((32, BLK), F32),
            pltpu.VMEM((n_dev, 32, BLK), F32),
            pltpu.VMEM((n_region, 32, BLK), F32),
            dma((4,)), dma((area_count,)), dma((peers,)), dma((peers,)), dma((groups,)), dma((groups,)), dma((groups,)),
            dma((n_dev,)), dma((n_region,)),
        ],
        compiler_params=pltpu.CompilerParams(
            collective_id=0, has_side_effects=True, vmem_limit_bytes=48 * 1024 * 1024
        ),
        name="admm",
    )(loads, factor, pivots, lower, upper, at.reshape(1, items), at.reshape(items, 1))
    return dispatch, duals.reshape(area_count, slots, BLK), res[:ITERS, :2]


def solution(mesh):
    placed = (
        P(("region", "dev"), None, None),
        P(("region", "dev"), None, None),
        P(("region", "dev"), None),
        P(("region", "dev"), None),
        P(("region", "dev"), None),
        P(("region", "dev"), None),
        P(("region", "dev")),
    )
    return jax.shard_map(
        on_device,
        mesh=mesh,
        in_specs=placed,
        out_specs=(P(("region", "dev"), None, None), P(("region", "dev"), None, None), P()),
        check_vma=False,
    )
```

```python
import functools

import jax
import jax.numpy as jnp
from jax import lax
from jax.experimental import pallas as pl
from jax.experimental.pallas import tpu as pltpu
from jax.sharding import PartitionSpec as P

ROWS_SLOT = 4
BLK = 128
BUS_DEV = 16
ITERS = 14
RHO = 4.0
SIGMA = 1.0
TILE = 256
F32 = jnp.float32
BF16 = jnp.bfloat16
MESH = pl.DeviceIdType.MESH
NT = (((1,), (1,)), ((), ()))
NN = (((1,), (0,)), ((), ()))


def mm(left, right, dims=NN):
    return lax.dot_general(left, right, dims, preferred_element_type=F32)


def split3(x):
    high = x.astype(BF16)
    rest = x - high.astype(F32)
    mid = rest.astype(BF16)
    low = (rest - mid.astype(F32)).astype(BF16)
    return high, mid, low


def kernel(
    n_region, n_dev, area_count, scenarios, order, slots,
    loads_hbm, factor_ref, pivots_hbm, lower_hbm, upper_hbm, row_ref, col_ref,
    dispatch_ref, duals_ref, res_ref,
    loads_ref, pivots_ref, lower_ref, upper_ref, fac, gram, diag, wide, edges, hot, known, known_b, diag_b, rounded, offset,
    pick, place, live, rhs_b, base_b, off_b, loads_b, low_b, up_b, blk, duals,
    part, got, table, mean, counts_got, members, res_sum, res_near, res_far,
    in_sem, fac_sem, send_sem, back_send, got_sem, table_sem, counts_sem, near_sem, far_sem,
):
    me_r = lax.axis_index("region")
    me_d = lax.axis_index("dev")
    items = area_count * slots
    rows = area_count * scenarios
    places = ROWS_SLOT * items
    edge = slots * ROWS_SLOT
    groups = n_dev + n_region
    near = [lax.rem(me_d + step, n_dev) for step in range(1, n_dev)]
    far = [lax.rem(me_r + step, n_region) for step in range(1, n_region)]
    peers = [((r, me_d), n_dev + r, n_dev + me_r, n_dev + r) for r in far]
    peers += [((me_r, d), d, me_d, d) for d in near]

    def factor_copy(area):
        return pltpu.make_async_copy(factor_ref.at[area], fac.at[area], fac_sem.at[area])

    inputs = [
        pltpu.make_async_copy(held, here, in_sem.at[number])
        for number, (held, here) in enumerate(
            ((loads_hbm, loads_ref), (pivots_hbm, pivots_ref), (lower_hbm, lower_ref), (upper_hbm, upper_ref))
        )
    ]
    for copy in inputs:
        copy.start()
    for area in range(area_count):
        factor_copy(area).start()

    got[...] = jnp.zeros_like(got)
    counts_got[...] = jnp.zeros_like(counts_got)
    table[...] = jnp.zeros_like(table)
    res_sum[...] = jnp.zeros_like(res_sum)

    barrier = pltpu.get_barrier_semaphore()
    for device, _, _, _ in peers:
        pl.semaphore_signal(barrier, inc=1, device_id=device, device_id_type=MESH)
    pl.semaphore_wait(barrier, len(peers))

    def group_rows(index):
        return pl.ds(pl.multiple_of(index * BUS_DEV, BUS_DEV), BUS_DEV)

    def outgoing(number, target, semaphores):
        device, theirs, mine, _ = peers[number]
        return pltpu.make_async_remote_copy(
            src_ref=part.at[group_rows(theirs)], dst_ref=target.at[group_rows(mine)],
            send_sem=send_sem.at[number], recv_sem=semaphores.at[mine],
            device_id=device, device_id_type=MESH,
        )

    def incoming(number, target, semaphores):
        device, theirs, _, here = peers[number]
        return pltpu.make_async_remote_copy(
            src_ref=part.at[group_rows(theirs)], dst_ref=target.at[group_rows(here)],
            send_sem=send_sem.at[number], recv_sem=semaphores.at[here],
            device_id=device, device_id_type=MESH,
        )

    def back(number, here=False):
        device, _, mine, theirs = peers[number]
        at = theirs if here else mine
        return pltpu.make_async_remote_copy(
            src_ref=mean, dst_ref=table.at[group_rows(at)],
            send_sem=back_send.at[number], recv_sem=table_sem.at[at],
            device_id=device, device_id_type=MESH,
        )

    def group_sum(ref):
        total = ref[0:BUS_DEV, :]
        for index in range(1, groups):
            total = total + ref[index * BUS_DEV : (index + 1) * BUS_DEV, :]
        return total

    picked = lax.broadcasted_iota(jnp.int32, (groups * BUS_DEV, items), 0) == row_ref[...]
    picked = jnp.where(picked, 1.0, 0.0)
    part[...] = jnp.broadcast_to(jnp.sum(picked, axis=1, keepdims=True), part.shape)
    for number in range(len(peers)):
        outgoing(number, counts_got, counts_sem).start()
    pick[...] = picked.astype(BF16)
    placed = lax.broadcasted_iota(jnp.int32, (items, groups * BUS_DEV), 1) == col_ref[...]
    place[...] = jnp.where(placed, 1.0, 0.0).astype(BF16)
    live[...] = jnp.broadcast_to(jnp.where(row_ref[...] >= 0, 1.0, 0.0), live.shape)
    counts_got[group_rows(me_d), :] = part[group_rows(me_d), :]

    def place_of(index):
        return lax.rem(index // slots, area_count), lax.rem(index, slots) * ROWS_SLOT + index // items

    source = lax.broadcasted_iota(jnp.int32, (area_count * BLK, places), 0)
    area_of, column_of = place_of(lax.broadcasted_iota(jnp.int32, (area_count * BLK, places), 1))
    hot[...] = jnp.where(source == area_of * BLK + column_of, 1.0, 0.0).astype(BF16)

    def stack_rows(x):
        return jnp.concatenate([x[:, r * items : (r + 1) * items] for r in range(ROWS_SLOT)], axis=0)

    def to_flat(x):
        parts = mm(jnp.concatenate(split3(x), axis=0), hot[...])
        return parts[:scenarios] + parts[scenarios : 2 * scenarios] + parts[2 * scenarios :]

    def line_flat(ref):
        line = jnp.concatenate([ref[a : a + 1, :BLK] for a in range(area_count)], axis=1)
        return to_flat(jnp.broadcast_to(line, (scenarios, area_count * BLK)))

    for copy in inputs:
        copy.wait()
    loads_b[...] = stack_rows(
        to_flat(jnp.concatenate([loads_ref[a, :, :BLK] for a in range(area_count)], axis=1))
    )
    low_b[...] = stack_rows(line_flat(lower_ref))
    up_b[...] = stack_rows(line_flat(upper_ref))

    tiles = order // TILE
    column = lax.broadcasted_iota(jnp.int32, (1, TILE), 1)
    cut = [slice(c * TILE, (c + 1) * TILE) for c in range(tiles)]

    for c in range(tiles):
        value = loads_ref[:, :, cut[c]].reshape(rows, TILE)
        if c == 0:
            value = jnp.where(column < edge, 0.0, value)
        rounded[:, cut[c]] = value.astype(BF16)

    same = lax.broadcasted_iota(jnp.int32, (BLK, BLK), 0) == lax.broadcasted_iota(jnp.int32, (BLK, BLK), 1)
    unit = jnp.where(same, 1.0, 0.0).astype(BF16)

    def forward_of(area):
        at = pl.ds(pl.multiple_of(area * scenarios, scenarios), scenarios)
        scaled = []
        for c in range(tiles):
            end = (c + 1) * TILE
            forward = mm(rounded[at, :end], fac[area, cut[c], :end], NT)
            scaled.append((forward * pivots_ref[pl.ds(area, 1), cut[c]]).astype(BF16))
        return jnp.concatenate(scaled, axis=1)

    def back_of(area, scaled):
        at = pl.ds(pl.multiple_of(area * scenarios, scenarios), scenarios)
        for c in range(tiles):
            known[at, cut[c]] = mm(scaled[:, c * TILE :], fac[area, c * TILE :, cut[c]])

    def product(pair, carry):
        first = forward_of(2 * pair)
        second = forward_of(2 * pair + 1)
        back_of(2 * pair, first)
        back_of(2 * pair + 1, second)
        return carry

    def form(area, carry):
        factor_copy(area).wait()
        pivot = pivots_ref[pl.ds(area, 1), :]
        flipped = (mm(unit, fac[area, :, :BLK], NT) * pivot).astype(BF16)
        for n in range(tiles):
            value = mm(flipped[:, n * TILE :], fac[area, n * TILE :, cut[n]])
            if n == 0:
                head = value[:, :BLK]
                exact = pivot[:, :BLK]
                found = jnp.sum(jnp.where(same, head, 0.0), axis=0, keepdims=True)
                diag[pl.ds(area, 1), :] = found - exact.astype(BF16).astype(F32) + exact
                value = jnp.concatenate([jnp.where(same, 0.0, head), value[:, BLK:]], axis=1)
            gram[area, :, cut[n]] = value.astype(BF16)
        back_of(area, forward_of(area))
        return carry

    lax.fori_loop(0, area_count, form, 0)

    target = lax.broadcasted_iota(jnp.int32, (places, area_count * BLK), 1)
    area_of, column_of = place_of(lax.broadcasted_iota(jnp.int32, (places, area_count * BLK), 0))
    hot_rows = jnp.where(target == area_of * BLK + column_of, 1.0, 0.0).astype(BF16)
    for c in range(tiles):
        joined = jnp.concatenate([gram[a, :, cut[c]] for a in range(area_count)], axis=0)
        wide[:, cut[c]] = mm(hot_rows, joined).astype(BF16)
    source = lax.broadcasted_iota(jnp.int32, (BLK, places), 0)
    _, column_of = place_of(lax.broadcasted_iota(jnp.int32, (BLK, places), 1))
    spread = jnp.where(source == column_of, 1.0, 0.0).astype(BF16)
    area_left, _ = place_of(lax.broadcasted_iota(jnp.int32, (places, places), 0))
    area_right, _ = place_of(lax.broadcasted_iota(jnp.int32, (places, places), 1))
    edges[...] = jnp.where(area_left == area_right, mm(wide[:, :BLK], spread), 0.0).astype(BF16)
    diag_b[...] = line_flat(diag)

    offset[...] = jnp.zeros_like(offset)
    off_b[...] = jnp.zeros_like(off_b)
    duals[...] = jnp.zeros_like(duals)
    mean[...] = jnp.zeros_like(mean)
    rhs_b[...] = loads_b[...]

    for number in range(len(peers)):
        incoming(number, counts_got, counts_sem).wait_recv()
        outgoing(number, counts_got, counts_sem).wait_send()
    members[...] = jnp.maximum(group_sum(counts_got), 1.0)

    own_area, _ = place_of(lax.broadcasted_iota(jnp.int32, (scenarios, places), 1))

    def known_edges():
        joined = [known[a * scenarios : (a + 1) * scenarios, :BLK] for a in range(area_count)]
        joined = jnp.concatenate(joined, axis=1)
        high = joined.astype(BF16)
        low = (joined - high.astype(F32)).astype(BF16)
        parts = mm(jnp.concatenate([high, low], axis=0), hot[...])
        known_b[...] = parts[:scenarios] + parts[scenarios:]

    known_edges()

    _, column_of = place_of(lax.broadcasted_iota(jnp.int32, (places, BLK), 0))
    back_hot = lax.broadcasted_iota(jnp.int32, (places, BLK), 1) == column_of
    back_hot = jnp.where(back_hot, 1.0, 0.0).astype(BF16)

    def iterate(step, carry):
        turned = rhs_b[...]
        flat = jnp.concatenate(
            [turned[r * scenarios : (r + 1) * scenarios, :] for r in range(ROWS_SLOT)], axis=1
        )
        flat = flat.astype(BF16)
        solved = known_b[...] + mm(flat, edges[...]) + flat.astype(F32) * diag_b[...]
        block = stack_rows(solved)
        blk[...] = block
        values = (block + duals[...]) * live[...]
        pieces = split3(values)
        part[...] = mm(pick[...], pieces[0], NT) + mm(pick[...], pieces[1], NT) + mm(pick[...], pieces[2], NT)
        for number in range(len(peers)):
            outgoing(number, got, got_sem).start()
        got[group_rows(me_d), :] = part[group_rows(me_d), :]
        moved = block + off_b[...]
        boxed = jnp.clip(moved, low_b[...], up_b[...])
        rest = moved - boxed
        off_b[...] = rest
        base_b[...] = loads_b[...] + SIGMA * (boxed - rest)

        left = jnp.concatenate(
            [jnp.where(own_area == a, flat.astype(F32), 0.0) for a in range(area_count)], axis=0
        ).astype(BF16)
        for c in range(tiles):
            found = known[:, cut[c]] + mm(left, wide[:, cut[c]])
            found = found.reshape(area_count, scenarios, TILE)
            dispatch_ref[:, :, cut[c]] = found
            moved = found + offset[:, :, cut[c]]
            boxed = jnp.clip(moved, lower_ref[:, cut[c]][:, None, :], upper_ref[:, cut[c]][:, None, :])
            rest = moved - boxed
            offset[:, :, cut[c]] = rest
            value = (loads_ref[:, :, cut[c]] + SIGMA * (boxed - rest)).reshape(rows, TILE)
            if c == 0:
                value = jnp.where(column < edge, 0.0, value)
            rounded[:, cut[c]] = value.astype(BF16)

        more = step < ITERS - 1

        @pl.when(step == ITERS - 1)
        def _():
            natural = mm(left, back_hot).reshape(area_count, scenarios, BLK) * diag[...][:, None, :]
            dispatch_ref[:, :, :BLK] = dispatch_ref[:, :, :BLK] + natural

        @pl.when(more)
        def _():
            lax.fori_loop(0, area_count // 4, product, 0)

        for number in range(len(peers)):
            incoming(number, got, got_sem).wait_recv()
        fresh = group_sum(got) / members[...]
        change = fresh - mean[...]
        mean[...] = fresh
        for number in range(len(peers)):
            back(number).start()
        table[group_rows(me_d), :] = fresh
        res_sum[pl.ds(16 + step, 1), :] = (RHO * RHO) * jnp.sum(change * change, axis=0, keepdims=True)

        @pl.when(more)
        def _():
            lax.fori_loop(area_count // 4, area_count // 2, product, 0)
            known_edges()

        for number in range(len(peers)):
            back(number, here=True).wait_recv()
        pieces = split3(table[...])
        z_slot = (mm(place[...], pieces[0]) + mm(place[...], pieces[1]) + mm(place[...], pieces[2])).T
        gap = (blk[...] - z_slot) * live[...]
        fresh_duals = duals[...] + gap
        duals[...] = fresh_duals
        rhs_b[...] = base_b[...] + RHO * (live[...] * (z_slot - fresh_duals))
        res_sum[pl.ds(step, 1), :] = jnp.sum(gap * gap, axis=0, keepdims=True)
        for number in range(len(peers)):
            outgoing(number, got, got_sem).wait_send()
            back(number).wait_send()
        return carry

    lax.fori_loop(0, ITERS, iterate, 0)

    def near_copy(number, here=False):
        device, _, mine, theirs = peers[number]
        at = theirs if here else mine
        return pltpu.make_async_remote_copy(
            src_ref=res_sum, dst_ref=res_near.at[at],
            send_sem=send_sem.at[number], recv_sem=near_sem.at[at], device_id=device, device_id_type=MESH,
        )

    def far_copy(number, here=False):
        device, _, mine, theirs = peers[number]
        at = (theirs if here else mine) - n_dev
        return pltpu.make_async_remote_copy(
            src_ref=res_sum, dst_ref=res_far.at[at],
            send_sem=send_sem.at[number], recv_sem=far_sem.at[at], device_id=device, device_id_type=MESH,
        )

    fars = range(n_region - 1)
    nears = range(n_region - 1, len(peers))
    for number in nears:
        near_copy(number).start()
    res_near[pl.ds(me_d, 1)] = res_sum[...][None]
    lane_from = lax.broadcasted_iota(jnp.int32, (BLK, BLK), 0)
    lane_to = lax.broadcasted_iota(jnp.int32, (BLK, BLK), 1)
    wanted = lax.rem(lane_to, ROWS_SLOT) * scenarios + lane_to // ROWS_SLOT
    lanes_hot = jnp.where(lane_from == wanted, 1.0, 0.0).astype(BF16)
    pieces = split3(duals[...].T)
    duals_ref[...] = mm(pieces[0], lanes_hot) + mm(pieces[1], lanes_hot) + mm(pieces[2], lanes_hot)
    for number in nears:
        near_copy(number, here=True).wait_recv()
        near_copy(number).wait_send()
    total = res_near[0]
    for index in range(1, n_dev):
        total = total + res_near[index]
    res_sum[...] = total
    for number in fars:
        far_copy(number).start()
    res_far[pl.ds(me_r, 1)] = total[None]
    for number in fars:
        far_copy(number, here=True).wait_recv()
        far_copy(number).wait_send()
    total = res_far[0]
    for index in range(1, n_region):
        total = total + res_far[index]
    sums = jnp.sum(total, axis=1, keepdims=True) / float(area_count * n_dev * n_region * BLK)
    lane = lax.broadcasted_iota(jnp.int32, (16, BLK), 1)
    res_ref[...] = jnp.where(lane == 0, sums[:16], sums[16:])


def on_device(loads, factor, pivots, lower, upper, incidence, counts):
    area_count, scenarios, order = loads.shape
    slots = incidence.shape[1]
    items = area_count * slots
    n_dev = lax.axis_size("dev")
    n_region = lax.axis_size("region")
    groups = n_dev + n_region
    peers = groups - 2
    table_rows = groups * BUS_DEV
    places = ROWS_SLOT * items
    rows = area_count * scenarios
    live_slot = jnp.arange(slots)[None, :] < counts[:, None]
    owner = incidence // BUS_DEV
    near = owner // n_dev == lax.axis_index("region")
    group = jnp.where(near, owner % n_dev, n_dev + owner // n_dev)
    at = jnp.where(live_slot, group * BUS_DEV + incidence % BUS_DEV, -1).astype(jnp.int32)

    vmem = pl.BlockSpec(memory_space=pltpu.VMEM)
    square = pltpu.VMEM((items, BLK), F32)
    bus = pltpu.VMEM((BUS_DEV, BLK), F32)
    listed = pltpu.VMEM((table_rows, BLK), F32)
    dma = pltpu.SemaphoreType.DMA
    dispatch, duals, res = pl.pallas_call(
        functools.partial(kernel, n_region, n_dev, area_count, scenarios, order, slots),
        out_shape=(
            jax.ShapeDtypeStruct(loads.shape, F32),
            jax.ShapeDtypeStruct((items, BLK), F32),
            jax.ShapeDtypeStruct((16, BLK), F32),
        ),
        in_specs=[pl.BlockSpec(memory_space=pltpu.HBM)] * 5 + [vmem] * 2,
        out_specs=(vmem, vmem, vmem),
        scratch_shapes=[
            pltpu.VMEM(loads.shape, F32),
            pltpu.VMEM(pivots.shape, F32),
            pltpu.VMEM(lower.shape, F32),
            pltpu.VMEM(upper.shape, F32),
            pltpu.VMEM((area_count, order, order), BF16),
            pltpu.VMEM((area_count, BLK, order), BF16),
            pltpu.VMEM((area_count, BLK), F32),
            pltpu.VMEM((places, order), BF16),
            pltpu.VMEM((places, places), BF16),
            pltpu.VMEM((area_count * BLK, places), BF16),
            pltpu.VMEM((rows, order), F32),
            pltpu.VMEM((scenarios, places), F32),
            pltpu.VMEM((scenarios, places), F32),
            pltpu.VMEM((rows, order), BF16),
            pltpu.VMEM(loads.shape, F32),
            pltpu.VMEM((table_rows, items), BF16),
            pltpu.VMEM((items, table_rows), BF16),
            square, square, square, square, square, square, square, square, square,
            listed, listed, listed, bus, listed, bus,
            pltpu.VMEM((32, BLK), F32),
            pltpu.VMEM((n_dev, 32, BLK), F32),
            pltpu.VMEM((n_region, 32, BLK), F32),
            dma((4,)), dma((area_count,)), dma((peers,)), dma((peers,)), dma((groups,)), dma((groups,)), dma((groups,)),
            dma((n_dev,)), dma((n_region,)),
        ],
        compiler_params=pltpu.CompilerParams(
            collective_id=0, has_side_effects=True, vmem_limit_bytes=48 * 1024 * 1024
        ),
        name="admm",
    )(loads, factor, pivots, lower, upper, at.reshape(1, items), at.reshape(items, 1))
    return dispatch, duals.reshape(area_count, slots, BLK), res[:ITERS, :2]


def solution(mesh):
    placed = (
        P(("region", "dev"), None, None),
        P(("region", "dev"), None, None),
        P(("region", "dev"), None),
        P(("region", "dev"), None),
        P(("region", "dev"), None),
        P(("region", "dev"), None),
        P(("region", "dev")),
    )
    return jax.shard_map(
        on_device,
        mesh=mesh,
        in_specs=placed,
        out_specs=(P(("region", "dev"), None, None), P(("region", "dev"), None, None), P()),
        check_vma=False,
    )
```
